512 devices in a mesh: grp: 16 (over y, x), shard: 32 (over z, core).
Axes of the slice: x: 4, y: 4, z: 16, core: 2. Of those that a mesh axis runs over, the one named last changes fastest.
Arguments:
- layer_input: bfloat16 [512, 128, 4096], P(('grp', 'shard')), may hold values from -6 to 6
- w_query: bfloat16 [4096, 64], replicated, may hold values from -0.01171875 to 0.01171875
- w_key: bfloat16 [4096, 64], replicated, may hold values from -0.09375 to 0.09375
- w_value: bfloat16 [4096, 64], replicated, may hold values from -0.09375 to 0.09375
- rel_bias: float32 [32], replicated, may hold values from -4 to 250
- context_grad: bfloat16 [512, 128, 64], P(('grp', 'shard')), may hold values from -1.5 to 1.5
- sign_bits: int32 [64, 3, 256], replicated, may hold values from 0 to 65535
- dither: int32 [512, 4096], P(('grp', 'shard')), may hold values from 0 to 65535
Outputs:
- mean_grad: float32 [64, 3, 4096], P('shard')
The draws below stay inside these ranges and needn't reach their ends.
Inputs may be any that keep to these rules, and one draw needn't show every extreme that they name: `sign_bits`: each word holds 16 sign bits; bit k of word w is the sign bit of entry 16 w + k of the block.
All inputs are finite; a program needn't handle non-finite values. Where the reference program divides by a largest or mean magnitude, that divisor is 1e-20 or more.
Results may differ from the reference program's by a relative error of at most 0.033.
The reference program's roundings to bfloat16 on the way (of `queries`, `probs_low`, `value_grad`, `score_grad` and `query_grad`) count: a program that leaves them out, or rounds other values in their place, can miss the bound.
Values sent between devices are 32-bit elements; how exact they have to be, the bound alone decides.
No kernel may reach another device: no remote copies, remote signals or barrier semaphores. Data moves between devices by JAX's collectives and lax.ppermute only.
A program may use at most 64 MiB of HBM per device.

```python
import math
import jax
import jax.numpy as jnp
from jax import lax

D = 4096
HD = 64
SEQ = 128
BUCKETS = 32
LEVELS = 64
BLOCK_SIDE = 64
BLOCK = 4096
BM = 64
BATCH = 512


def draw_rel_bias(key, part):
    key = jax.random.fold_in(key, 7)
    first_key = jax.random.fold_in(key, 0)
    return jnp.clip(jax.random.normal(first_key, (BUCKETS,), jnp.float32), -4.0, 4.0)


def touch_ends(result, key, least, top_value):
    index_at = [jax.random.randint(jax.random.fold_in(key, axis), (), 0, length) for axis, length in enumerate(result.shape)]
    widest = result.shape.index(max(result.shape))
    beside = index_at[:widest] + [(index_at[widest] + 1) % result.shape[widest]] + index_at[widest + 1:]
    return result.at[tuple(index_at)].set(least).at[tuple(beside)].set(top_value)


def steps_of(key, extent, cuts, low, largest):
    loudness = 1.0
    for dim, blocks in cuts:
        draws = jax.random.uniform(jax.random.fold_in(jax.random.fold_in(key, 6), dim), (blocks,), jnp.float32, low / len(cuts), largest / len(cuts))
        loudness = loudness * jnp.repeat(jnp.exp(draws), extent[dim] // blocks).reshape((-1,) + (1,) * (len(extent) - 1 - dim))
    return loudness


def bell_draw(stream_key, dims, deviation, most, shards=(), kind=jnp.bfloat16):
    drawn = jax.random.normal(stream_key, dims, jnp.float32) * deviation
    if len(shards) > 0:
        drawn = steps_of(stream_key, dims, shards, -0.22, 0.18) * drawn
    return jnp.clip(drawn, min=-most, max=most).astype(kind)


def setup_inputs(seed: int = 0) -> dict:
    streams_of = jax.random.split(jax.random.key(seed), 9)
    return {
        "layer_input": bell_draw(streams_of[0], (BATCH, SEQ, D), 1.0, 6.0, ((0, 512),)),
        "w_query": bell_draw(streams_of[1], (D, HD), (D * HD) ** -0.5, 0.01171875),
        "w_key": bell_draw(streams_of[2], (D, HD), D ** -0.5, 0.09375),
        "w_value": bell_draw(streams_of[3], (D, HD), D ** -0.5, 0.09375),
        "rel_bias": draw_rel_bias(jax.random.fold_in(streams_of[8], 71), 0),
        "context_grad": bell_draw(streams_of[5], (BATCH, SEQ, HD), 0.1, 1.5, ((0, 512),)),
        "sign_bits": touch_ends(jax.random.randint(streams_of[6], (BM, 3, BLOCK // 16), 0, 65536), jax.random.fold_in(streams_of[6], 1), 0, 65535).astype(jnp.int32),
        "dither": touch_ends(jax.random.randint(streams_of[7], (BATCH, BLOCK), 0, 65536), jax.random.fold_in(streams_of[7], 1), 0, 65535).astype(jnp.int32),
    }


EPS = 1e-06
THRESHOLDS = (12, 16, 23, 32, 46, 64, 91)

def sylvester(side_len):
    counter = jnp.arange(side_len, dtype=jnp.int32)
    common = jnp.bitwise_and(counter[:, None], counter[None, :])
    parity = jnp.zeros((side_len, side_len), jnp.int32)
    for bit_index in range(side_len.bit_length() - 1):
        parity = parity + jnp.bitwise_and(jnp.right_shift(common, bit_index), 1)
    return (1 - 2 * (parity % 2)).astype(jnp.float32) / math.sqrt(side_len)

def decode_signs(sign_bits):
    bit_shifts = jnp.arange(16, dtype=jnp.int32)
    bit_values = jnp.bitwise_and(jnp.right_shift(sign_bits[..., None], bit_shifts), 1)
    flat_bits = bit_values.reshape(sign_bits.shape[:-1] + (sign_bits.shape[-1] * 16,))
    return 1.0 - 2.0 * flat_bits.astype(jnp.float32)

def rotate_blocks(blocks, signs, table, side_len):
    grid = (blocks * signs).reshape(blocks.shape[:-1] + (side_len, side_len))
    mixed = jnp.einsum('ab,...bc,cd->...ad', table, grid, table, precision=lax.Precision.HIGHEST)
    return mixed.reshape(blocks.shape)

def unrotate_blocks(blocks, signs, table, side_len):
    grid = blocks.reshape(blocks.shape[:-1] + (side_len, side_len))
    mixed = jnp.einsum('ab,...bc,cd->...ad', table, grid, table, precision=lax.Precision.HIGHEST)
    return mixed.reshape(blocks.shape) * signs

def bias_matrix(rel_bias, length):
    offsets = jnp.arange(-(length - 1), length, dtype=jnp.int32)
    distance = jnp.abs(offsets)
    far_bucket = jnp.full(distance.shape, 8, jnp.int32)
    for limit in THRESHOLDS:
        far_bucket = far_bucket + (distance >= limit).astype(jnp.int32)
    bucket = jnp.where(distance < 8, distance, far_bucket) + 16 * (offsets > 0).astype(jnp.int32)
    one_hot = (bucket[:, None] == jnp.arange(rel_bias.shape[0], dtype=jnp.int32)[None, :]).astype(jnp.float32)
    offset_bias = jnp.dot(one_hot, rel_bias, precision=lax.Precision.HIGHEST)
    position = jnp.arange(length, dtype=jnp.int32)
    index_table = position[None, :] - position[:, None] + (length - 1)
    return jnp.take(offset_bias, index_table)

def head_grads(inputs, upstream, w_query, w_key, w_value, bias_mat):
    queries = jnp.dot(inputs, w_query, preferred_element_type=jnp.float32).astype(jnp.bfloat16)
    key_rows = jnp.dot(inputs, w_key, preferred_element_type=jnp.float32).astype(jnp.bfloat16)
    value_rows = jnp.dot(inputs, w_value, preferred_element_type=jnp.float32).astype(jnp.bfloat16)
    scores = jnp.dot(queries, key_rows.T, preferred_element_type=jnp.float32) + bias_mat
    top_score = lax.optimization_barrier(jnp.max(scores, axis=1, keepdims=True))
    weights = jnp.exp(scores - top_score)
    probs = weights / lax.optimization_barrier(jnp.sum(weights, axis=1, keepdims=True))
    probs_low = probs.astype(jnp.bfloat16)
    value_grad = jnp.dot(probs_low.T, upstream, preferred_element_type=jnp.float32).astype(jnp.bfloat16)
    prob_grad = jnp.dot(upstream, value_rows.T, preferred_element_type=jnp.float32)
    score_grad = (probs * (prob_grad - lax.optimization_barrier(jnp.sum(probs * prob_grad, axis=1, keepdims=True)))).astype(jnp.bfloat16)
    query_grad = jnp.dot(score_grad, key_rows, preferred_element_type=jnp.float32).astype(jnp.bfloat16)
    key_grad = jnp.dot(score_grad.T, queries, preferred_element_type=jnp.float32).astype(jnp.bfloat16)
    return jnp.stack([jnp.dot(inputs.T, query_grad, preferred_element_type=jnp.float32), jnp.dot(inputs.T, key_grad, preferred_element_type=jnp.float32), jnp.dot(inputs.T, value_grad, preferred_element_type=jnp.float32)])

def reference(layer_input, w_query, w_key, w_value, rel_bias, context_grad, sign_bits, dither):
    side_len = BLOCK_SIDE
    table = sylvester(side_len)
    signs = decode_signs(sign_bits)
    bias_mat = bias_matrix(rel_bias, SEQ)

    def one_device(pair):
        inputs, upstream = pair
        grads = head_grads(inputs, upstream, w_query, w_key, w_value, bias_mat)
        blocks = grads.reshape(3, BM, BLOCK).transpose(1, 0, 2)
        return rotate_blocks(blocks, signs, table, side_len)
    rotated = lax.map(one_device, (layer_input, context_grad))
    peaks = lax.optimization_barrier(jnp.max(jnp.abs(rotated), axis=(0, 3)))
    factor = LEVELS / (peaks + EPS)
    dither_shift = (dither.astype(jnp.float32) + 0.5) / 65536.0

    def add_codes(total, pair):
        rotated_one, shift_one = pair
        return (total + jnp.floor(rotated_one * factor[..., None] + shift_one), None)
    totals, _ = lax.scan(add_codes, jnp.zeros((BM, 3, BLOCK), jnp.float32), (rotated, dither_shift))
    decoded = totals * ((peaks + EPS) / LEVELS)[..., None] / BATCH
    return unrotate_blocks(decoded, signs, table, side_len)
```

```python
import jax
import jax.numpy as jnp
from jax import lax
from jax.experimental import pallas as pl
from jax.experimental.pallas import tpu as pltpu
from jax.sharding import PartitionSpec as P

LEVELS = 64
EPS = 1e-06
THRESHOLDS = (12, 16, 23, 32, 46, 64, 91)
SEQ, D, HD = 128, 4096, 64
SIDE = 64
GRP, ZS = 16, 16
BATCH = 512
ROWS = 3 * ZS
F32, BF16, I32 = jnp.float32, jnp.bfloat16, jnp.int32
NT = (((1,), (1,)), ((), ()))


def iota(shape, dim):
    return lax.broadcasted_iota(I32, shape, dim)


def parity(v):
    v = v ^ (v >> 4)
    v = v ^ (v >> 2)
    v = v ^ (v >> 1)
    return v & 1


def hadamard(size, swap=0):
    row, col = iota((size, size), 0), iota((size, size), 1)
    value = (1 - 2 * parity(row & col & (SIDE - 1))).astype(F32) * 0.125
    same = (row >> 6) == ((col >> 6) ^ (swap * 2))
    return jnp.where(same, value, 0.0).astype(BF16)


def mm(a, b):
    return jnp.dot(a, b, preferred_element_type=F32)


def terms(v, count):
    out = []
    for _ in range(count):
        part = v.astype(BF16)
        out.append(part)
        v = v - part.astype(F32)
    return out


def rotate(grid, left, right, count):
    mixed = sum(mm(t, right) for t in terms(grid, count))
    return sum(mm(left, t) for t in terms(mixed, count))


def grads_kernel(x_ref, wq_ref, wk_ref, wv_ref, bias_ref, ctx_ref, bits_ref, dither_ref,
                 mine_ref, send_ref, peaks_ref, words_ref, word_scr, peak_scr, bits_scr):
    shard = lax.axis_index("shard")
    core = shard & 1
    depth = shard >> 1

    for p in range(3):
        for part in (0, 1):
            bits_scr[2 * p + part] = bits_ref[p, :, part * 128:part * 128 + 128]
    rows = []
    for half in (0, 1):
        for p in range(3):
            rows.append(jnp.concatenate(
                [bits_scr[2 * p + part, pl.ds(2 * half + b, ZS, stride=4), :]
                 for b in (0, 1) for part in (0, 1)], axis=1))
    words = jnp.concatenate(rows, axis=0)
    both = jnp.concatenate([words & 255, words >> 8], axis=0).astype(F32).astype(BF16)
    row, col = iota((512, 512), 0), iota((512, 512), 1)
    source = ((col >> 6) & 1) * 256 + (col & 63) * 4 + (col >> 7)
    select = jnp.where(row == source, 1.0, 0.0).astype(BF16)
    moved = mm(both, select)
    moved = (moved[:96] + 256.0 * moved[96:]).astype(I32)
    for half in (0, 1):
        for j in range(4):
            word_scr[:, j * 256 + half * 128:j * 256 + half * 128 + 128] = (
                moved[half * 48:half * 48 + 48, j * 128:j * 128 + 128])
    for p in range(3):
        for j in range(4):
            own = word_scr[pl.ds(p * ZS + depth, 1), j * 256:j * 256 + 256]
            words_ref[p, j:j + 1, :] = jnp.where(core == 0, own[:, :128], own[:, 128:])

    shift = (dither_ref[...].astype(F32) + 0.5) * (1.0 / 65536.0)
    shift = shift.T
    shift = jnp.concatenate([shift, shift], axis=1)
    mine_ref[ROWS] = shift
    send_ref[ROWS] = shift

    acc = jnp.zeros((SEQ, 3 * HD), F32)
    step = 512
    for k in range(0, D, step):
        w = jnp.concatenate([r[k:k + step, :] for r in (wq_ref, wk_ref, wv_ref)], axis=1)
        acc = acc + mm(x_ref[:, k:k + step], w)
    q32 = acc[:, :HD].astype(BF16).astype(F32)
    k32 = acc[:, HD:2 * HD].astype(BF16).astype(F32)
    queries, keys, values = (q32.astype(BF16), k32.astype(BF16), acc[:, 2 * HD:].astype(BF16))
    upstream = ctx_ref[...]
    offset = iota((SEQ, SEQ), 1) - iota((SEQ, SEQ), 0)
    distance = jnp.abs(offset)
    bucket = jnp.minimum(distance, 8)
    for limit in THRESHOLDS:
        bucket = bucket + (distance >= limit).astype(I32)
    bucket = bucket + jnp.where(offset > 0, 16, 0)
    bias = jnp.zeros((SEQ, SEQ), F32)
    for b in range(32):
        bias = jnp.where(bucket == b, bias_ref[b], bias)
    scores = lax.dot_general(queries, keys, NT, preferred_element_type=F32) + bias
    weights = jnp.exp(scores - jnp.max(scores, axis=1, keepdims=True))
    probs = weights / jnp.sum(weights, axis=1, keepdims=True)
    prob_grad = lax.dot_general(upstream, values, NT, preferred_element_type=F32)
    score_grad = (probs * (prob_grad - jnp.sum(probs * prob_grad, axis=1, keepdims=True))).astype(BF16)
    query_grad = lax.dot_general(k32.T.astype(BF16), score_grad, NT, preferred_element_type=F32)
    key_grad = mm(q32.T.astype(BF16), score_grad)
    value_grad = mm(upstream.astype(F32).T.astype(BF16), probs.astype(BF16))
    stacked = jnp.concatenate([query_grad, key_grad, value_grad], axis=0).astype(BF16)

    left = hadamard(192)
    right = hadamard(256, core)
    bit = iota((16, 256), 0)
    for z in range(ZS):
        grid = mm(stacked, x_ref[:, 256 * z:256 * z + 256])
        signed = []
        for p in range(3):
            for j in range(4):
                line = word_scr[p * ZS + z:p * ZS + z + 1, j * 256:j * 256 + 256]
                flip = (jnp.broadcast_to(line, (16, 256)) >> bit) & 1
                part = grid[p * 64 + j * 16:p * 64 + j * 16 + 16, :]
                signed.append(jnp.where(flip == 1, -part, part))
        turned = rotate(jnp.concatenate(signed, axis=0), left, right, 2)
        for p in range(3):
            block = turned[p * 64:p * 64 + 64, :]
            mine_ref[3 * z + p] = block[:, :128]
            send_ref[3 * z + p] = block[:, 128:]
            peak_scr[3 * z + p:3 * z + p + 1, :] = jnp.max(jnp.abs(block), axis=0, keepdims=True)
    lane, line = iota((ROWS, 128), 1), iota((ROWS, 128), 0)
    for half in (0, 1):
        peaks = peak_scr[:, half * 128:half * 128 + 128]
        low = jnp.max(jnp.where(lane < 64, peaks, 0.0), axis=1, keepdims=True)
        high = jnp.max(jnp.where(lane >= 64, peaks, 0.0), axis=1, keepdims=True)
        spread = jnp.where(lane == line, low, 0.0) + jnp.where(lane - 64 == line, high, 0.0)
        packed = jnp.max(spread, axis=0, keepdims=True)
        for z in range(ZS):
            peaks_ref[2 * z + (core ^ half)] = packed


def codes_kernel(mine_ref, other_ref, peaks_ref, out_ref):
    factor = LEVELS / (jnp.max(peaks_ref[...], axis=0) + EPS)
    lane, line = iota((ROWS, 128), 1), iota((ROWS, 128), 0)
    low = jnp.sum(jnp.where(lane == line, factor, 0.0), axis=1, keepdims=True)
    high = jnp.sum(jnp.where(lane - 64 == line, factor, 0.0), axis=1, keepdims=True)
    factor = jnp.where(lane < 64, low, high)
    for t in range(ROWS):
        f = factor[t:t + 1, :]
        codes = (jnp.floor(mine_ref[t] * f + mine_ref[ROWS])
                 + jnp.floor(other_ref[t] * f + other_ref[ROWS]))
        for q in range(GRP):
            out_ref[q, t] = codes[4 * q:4 * q + 4, :]


def decode_kernel(totals_ref, peaks_ref, words_ref, out_ref, scr):
    depth = lax.axis_index("shard") >> 1
    step = (jnp.max(peaks_ref[...], axis=0) + EPS) / LEVELS
    lane = iota((1, 128), 1)
    grids, signs = [], []
    bit = iota((16, 128), 0)
    for p in range(3):
        low = jnp.sum(jnp.where(lane == 3 * depth + p, step, 0.0), axis=1, keepdims=True)
        high = jnp.sum(jnp.where(lane - 64 == 3 * depth + p, step, 0.0), axis=1, keepdims=True)
        total = jnp.concatenate([totals_ref[q, p] for q in range(GRP)], axis=0)
        grids.append(total * jnp.where(lane < 64, low, high) / BATCH)
        for j in range(4):
            word = jnp.broadcast_to(words_ref[p, j:j + 1, :], (16, 128))
            signs.append((word >> bit) & 1)
    mixed = rotate(jnp.concatenate(grids, axis=0), hadamard(192), hadamard(128), 3)
    mixed = jnp.where(jnp.concatenate(signs, axis=0) == 1, -mixed, mixed)
    for p in range(3):
        turned = mixed[64 * p:64 * p + 64, :].T
        scr[...] = jnp.concatenate([turned, turned], axis=1)
        for b in (0, 1):
            pair = [scr[pl.ds(64 * b + odd, 32, stride=2), :][:, :SIDE] for odd in (0, 1)]
            lines = jnp.concatenate(pair, axis=1)
            for r in range(32):
                out_ref[b, p:p + 1, 128 * r:128 * r + 128] = lines[r:r + 1, :]


def vmem(count):
    return [pl.BlockSpec(memory_space=pltpu.VMEM)] * count


def shaped(*shape, dtype=F32):
    return jax.ShapeDtypeStruct(shape, dtype)


PARAMS = pltpu.CompilerParams(vmem_limit_bytes=40 * 1024 * 1024)


def per_device(layer_input, w_query, w_key, w_value, rel_bias, context_grad, sign_bits, dither):
    in_specs = vmem(8)
    in_specs[4] = pl.BlockSpec(memory_space=pltpu.SMEM)
    mine, send, peaks, words = pl.pallas_call(
        grads_kernel,
        out_shape=[shaped(ROWS + 1, SIDE, 128), shaped(ROWS + 1, SIDE, 128),
                   shaped(2 * ZS, 1, 128), shaped(3, 4, 128, dtype=I32)],
        in_specs=in_specs,
        out_specs=vmem(4),
        scratch_shapes=[pltpu.VMEM((ROWS, 1024), I32), pltpu.VMEM((ROWS, 256), F32),
                        pltpu.VMEM((6, SIDE, 128), I32)],
        compiler_params=PARAMS,
        name="grads",
    )(layer_input[0], w_query, w_key, w_value, rel_bias, context_grad[0],
      sign_bits.transpose(1, 0, 2), dither.reshape(SIDE, SIDE))
    other = lax.ppermute(send, "shard", [(i, i ^ 1) for i in range(2 * ZS)])
    peaks = jnp.max(lax.all_to_all(peaks, "shard", 0, 0), axis=0)
    peaks = lax.all_to_all(jnp.broadcast_to(peaks, (GRP, 1, 128)), "grp", 0, 0)
    codes = pl.pallas_call(
        codes_kernel,
        out_shape=shaped(GRP, ROWS, 4, 128),
        in_specs=vmem(3),
        out_specs=vmem(1)[0],
        compiler_params=PARAMS,
        name="codes",
    )(mine, other, peaks)
    part = jnp.sum(lax.all_to_all(codes, "grp", 0, 0), axis=0).reshape(ZS, 3, 4, 128)
    same_core = [list(range(c, 2 * ZS, 2)) for c in (0, 1)]
    part = jnp.sum(lax.all_to_all(part, "shard", 0, 0, axis_index_groups=same_core), axis=0)
    totals = lax.all_to_all(jnp.broadcast_to(part, (GRP, 3, 4, 128)), "grp", 0, 0)
    return pl.pallas_call(
        decode_kernel,
        out_shape=shaped(2, 3, SIDE * SIDE),
        in_specs=vmem(3),
        out_specs=vmem(1)[0],
        scratch_shapes=[pltpu.VMEM((128, 128), F32)],
        compiler_params=PARAMS,
        name="decode",
    )(totals, peaks, words)


def solution(mesh):
    batch = P(("grp", "shard"), None, None)
    placed = (batch, P(), P(), P(), P(), batch, P(), P(("grp", "shard"), None))
    return jax.shard_map(
        per_device, mesh=mesh, in_specs=placed, out_specs=P("shard", None, None), check_vma=False
    )
```

```python
import jax
import jax.numpy as jnp
from jax import lax
from jax.experimental import pallas as pl
from jax.experimental.pallas import tpu as pltpu
from jax.sharding import PartitionSpec as P

LEVELS = 64
EPS = 1e-06
THRESHOLDS = (12, 16, 23, 32, 46, 64, 91)
SEQ, D, HD = 128, 4096, 64
SIDE = 64
GRP, ZS = 16, 16
BATCH = 512
ROWS = 3 * ZS
X_STEP = 1024
F32, BF16, I32 = jnp.float32, jnp.bfloat16, jnp.int32
NT = (((1,), (1,)), ((), ()))


def iota(shape, dim):
    return lax.broadcasted_iota(I32, shape, dim)


def parity(v):
    v = v ^ (v >> 4)
    v = v ^ (v >> 2)
    v = v ^ (v >> 1)
    return v & 1


def hadamard(size, swap=0):
    row, col = iota((size, size), 0), iota((size, size), 1)
    value = (1 - 2 * parity(row & col & (SIDE - 1))).astype(F32) * 0.125
    same = (row >> 6) == ((col >> 6) ^ (swap * 2))
    return jnp.where(same, value, 0.0).astype(BF16)


def mm(a, b):
    return jnp.dot(a, b, preferred_element_type=F32)


def terms(v, count):
    out = []
    for _ in range(count):
        part = v.astype(BF16)
        out.append(part)
        v = v - part.astype(F32)
    return out


def rotate(grid, left, right, count):
    mixed = sum(mm(t, right) for t in terms(grid, count))
    return sum(mm(left, t) for t in terms(mixed, count))


def grads_kernel(x_ref, wq_ref, wk_ref, wv_ref, bias_in, ctx_in, bits_in, dither_in,
                 mine_out, send_out, peaks_ref, words_ref, word_scr, peak_scr, bits_scr,
                 dither_scr, grid_scr, x_scr, w_scr, bits_ref, bias_ref, dither_ref, ctx_ref,
                 mine_ref, send_ref, x_sem, w_sem, in_sem, out_sem):
    shard = lax.axis_index("shard")
    core = shard & 1
    depth = shard >> 1
    w_copies = [pltpu.make_async_copy(r, w_scr.at[pl.ds(HD * n, HD)], w_sem.at[n])
                for n, r in enumerate((wq_ref, wk_ref, wv_ref))]
    x_copies = [pltpu.make_async_copy(x_ref.at[:, pl.ds(n * X_STEP, X_STEP)],
                                      x_scr.at[:, pl.ds(n * X_STEP, X_STEP)], x_sem.at[n])
                for n in range(D // X_STEP)]
    sent = []

    def ship(start, count, slot):
        rows = pl.ds(start, count)
        for n, (src, dst) in enumerate(((mine_ref, mine_out), (send_ref, send_out))):
            copy = pltpu.make_async_copy(src.at[rows], dst.at[rows], out_sem.at[n, slot])
            copy.start()
            sent.append(copy)

    small = [pltpu.make_async_copy(src, dst, in_sem.at[n]) for n, (src, dst) in enumerate(
        ((bits_in, bits_ref), (bias_in, bias_ref), (dither_in, dither_ref), (ctx_in, ctx_ref)))]
    for copy in small + w_copies + x_copies:
        copy.start()
    small[0].wait()

    for p in range(3):
        for part in (0, 1):
            bits_scr[2 * p + part] = bits_ref[p, :, part * 128:part * 128 + 128]
    rows = []
    for half in (0, 1):
        for p in range(3):
            rows.append(jnp.concatenate(
                [bits_scr[2 * p + part, pl.ds(2 * half + b, ZS, stride=4), :]
                 for b in (0, 1) for part in (0, 1)], axis=1))
    words = jnp.concatenate(rows, axis=0)
    both = jnp.concatenate([words & 255, words >> 8], axis=0).astype(F32).astype(BF16)
    row, col = iota((512, 512), 0), iota((512, 512), 1)
    source = ((col >> 6) & 1) * 256 + (col & 63) * 4 + (col >> 7)
    select = jnp.where(row == source, 1.0, 0.0).astype(BF16)
    moved = mm(both, select)
    moved = (moved[:96] + 256.0 * moved[96:]).astype(I32)
    for half in (0, 1):
        for j in range(4):
            word_scr[:, j * 256 + half * 128:j * 256 + half * 128 + 128] = (
                moved[half * 48:half * 48 + 48, j * 128:j * 128 + 128])
    for p in range(3):
        for j in range(4):
            own = word_scr[pl.ds(p * ZS + depth, 1), j * 256:j * 256 + 256]
            words_ref[p, j:j + 1, :] = jnp.where(core == 0, own[:, :128], own[:, 128:])

    for copy in small[1:]:
        copy.wait()
    for r in range(32):
        dither_scr[r:r + 1, :] = dither_ref[:, 128 * r:128 * r + 128]
    even = dither_scr[...]
    grid_scr[pl.ds(0, 32, stride=2), :] = even
    grid_scr[pl.ds(1, 32, stride=2), :] = pltpu.roll(even, SIDE, 1)
    shift = ((grid_scr[...].astype(F32) + 0.5) * (1.0 / 65536.0)).T[:SIDE, :]
    shift = jnp.concatenate([shift, shift], axis=1)
    mine_ref[ROWS] = shift
    send_ref[ROWS] = shift
    ship(ROWS, 1, ZS)

    acc = jnp.zeros((3 * HD, SEQ), F32)
    for copy in w_copies:
        copy.wait()
    for n, copy in enumerate(x_copies):
        copy.wait()
        for k in range(n * X_STEP, n * X_STEP + X_STEP, 512):
            acc = acc + lax.dot_general(w_scr[:, k:k + 512], x_scr[:, k:k + 512], NT,
                                        preferred_element_type=F32)
    queries_t, keys_t, values_t = (acc[HD * n:HD * n + HD, :].astype(BF16) for n in range(3))
    queries = acc[:HD, :].T.astype(BF16)
    upstream_t = ctx_ref[...]
    upstream = upstream_t.astype(F32).T.astype(BF16)
    offset = iota((SEQ, SEQ), 1) - iota((SEQ, SEQ), 0)
    distance = jnp.abs(offset)
    bucket = jnp.minimum(distance, 8)
    for limit in THRESHOLDS:
        bucket = bucket + (distance >= limit).astype(I32)
    bucket = bucket + jnp.where(offset > 0, 16, 0)
    bias = jnp.zeros((SEQ, SEQ), F32)
    for b in range(32):
        bias = jnp.where(bucket == b, bias_ref[b], bias)
    scores = mm(queries, keys_t) + bias
    weights = jnp.exp(scores - jnp.max(scores, axis=1, keepdims=True))
    probs = weights / jnp.sum(weights, axis=1, keepdims=True)
    prob_grad = mm(upstream, values_t)
    score_grad = (probs * (prob_grad - jnp.sum(probs * prob_grad, axis=1, keepdims=True))).astype(BF16)
    query_grad = lax.dot_general(keys_t, score_grad, NT, preferred_element_type=F32)
    key_grad = mm(queries_t, score_grad)
    value_grad = mm(upstream_t, probs.astype(BF16))
    stacked = jnp.concatenate([query_grad, key_grad, value_grad], axis=0).astype(BF16)

    left = hadamard(192)
    right = hadamard(256, core)
    bit = iota((16, 256), 0)
    for z in range(ZS):
        grid = mm(stacked, x_scr[:, 256 * z:256 * z + 256])
        signed = []
        for p in range(3):
            for j in range(4):
                line = word_scr[p * ZS + z:p * ZS + z + 1, j * 256:j * 256 + 256]
                flip = (jnp.broadcast_to(line, (16, 256)) >> bit) & 1
                part = grid[p * 64 + j * 16:p * 64 + j * 16 + 16, :]
                signed.append(jnp.where(flip == 1, -part, part))
        turned = rotate(jnp.concatenate(signed, axis=0), left, right, 2)
        for p in range(3):
            block = turned[p * 64:p * 64 + 64, :]
            mine_ref[3 * z + p] = block[:, :128]
            send_ref[3 * z + p] = block[:, 128:]
            peak_scr[3 * z + p:3 * z + p + 1, :] = jnp.max(jnp.abs(block), axis=0, keepdims=True)
        ship(3 * z, 3, z)
    lane, line = iota((ROWS, 128), 1), iota((ROWS, 128), 0)
    for half in (0, 1):
        peaks = peak_scr[:, half * 128:half * 128 + 128]
        low = jnp.max(jnp.where(lane < 64, peaks, 0.0), axis=1, keepdims=True)
        high = jnp.max(jnp.where(lane >= 64, peaks, 0.0), axis=1, keepdims=True)
        spread = jnp.where(lane == line, low, 0.0) + jnp.where(lane - 64 == line, high, 0.0)
        packed = jnp.max(spread, axis=0, keepdims=True)
        for z in range(ZS):
            peaks_ref[2 * z + (core ^ half)] = packed
    for copy in sent:
        copy.wait()


def codes_kernel(mine_ref, other_ref, peaks_ref, out_ref):
    factor = LEVELS / (jnp.max(peaks_ref[...], axis=0) + EPS)
    lane, line = iota((ROWS, 128), 1), iota((ROWS, 128), 0)
    low = jnp.sum(jnp.where(lane == line, factor, 0.0), axis=1, keepdims=True)
    high = jnp.sum(jnp.where(lane - 64 == line, factor, 0.0), axis=1, keepdims=True)
    factor = jnp.where(lane < 64, low, high)
    for t in range(ROWS):
        f = factor[t:t + 1, :]
        codes = (jnp.floor(mine_ref[t] * f + mine_ref[ROWS])
                 + jnp.floor(other_ref[t] * f + other_ref[ROWS]))
        for q in range(GRP):
            out_ref[q, t] = codes[4 * q:4 * q + 4, :]


def decode_kernel(totals_ref, peaks_ref, words_ref, out_ref, scr):
    depth = lax.axis_index("shard") >> 1
    step = (jnp.max(peaks_ref[...], axis=0) + EPS) / LEVELS
    lane = iota((1, 128), 1)
    grids, signs = [], []
    bit = iota((16, 128), 0)
    for p in range(3):
        low = jnp.sum(jnp.where(lane == 3 * depth + p, step, 0.0), axis=1, keepdims=True)
        high = jnp.sum(jnp.where(lane - 64 == 3 * depth + p, step, 0.0), axis=1, keepdims=True)
        total = jnp.concatenate([totals_ref[q, p] for q in range(GRP)], axis=0)
        grids.append(total * jnp.where(lane < 64, low, high) / BATCH)
        for j in range(4):
            word = jnp.broadcast_to(words_ref[p, j:j + 1, :], (16, 128))
            signs.append((word >> bit) & 1)
    mixed = rotate(jnp.concatenate(grids, axis=0), hadamard(192), hadamard(128), 3)
    mixed = jnp.where(jnp.concatenate(signs, axis=0) == 1, -mixed, mixed)
    for p in range(3):
        turned = mixed[64 * p:64 * p + 64, :].T
        scr[...] = jnp.concatenate([turned, turned], axis=1)
        for b in (0, 1):
            pair = [scr[pl.ds(64 * b + odd, 32, stride=2), :][:, :SIDE] for odd in (0, 1)]
            lines = jnp.concatenate(pair, axis=1)
            for r in range(32):
                out_ref[p, b:b + 1, 128 * r:128 * r + 128] = lines[r:r + 1, :]


def vmem(count):
    return [pl.BlockSpec(memory_space=pltpu.VMEM)] * count


def shaped(*shape, dtype=F32):
    return jax.ShapeDtypeStruct(shape, dtype)


PARAMS = pltpu.CompilerParams(vmem_limit_bytes=16 * 1024 * 1024)


def per_device(layer_input, w_query, w_key, w_value, rel_bias, context_grad, sign_bits, dither):
    mine, send, peaks, words = pl.pallas_call(
        grads_kernel,
        out_shape=[shaped(ROWS + 1, SIDE, 128), shaped(ROWS + 1, SIDE, 128),
                   shaped(2 * ZS, 1, 128), shaped(3, 4, 128, dtype=I32)],
        in_specs=[pl.BlockSpec(memory_space=pltpu.HBM)] * 8,
        out_specs=[pl.BlockSpec(memory_space=pltpu.HBM)] * 2 + vmem(2),
        scratch_shapes=[pltpu.VMEM((ROWS, 1024), I32), pltpu.VMEM((ROWS, 256), F32),
                        pltpu.VMEM((6, SIDE, 128), I32),
                        pltpu.VMEM((32, 128), I32), pltpu.VMEM((SIDE, 128), I32),
                        pltpu.VMEM((SEQ, D), BF16), pltpu.VMEM((3 * HD, D), BF16),
                        pltpu.VMEM((3, SIDE, 256), I32), pltpu.SMEM((32,), F32),
                        pltpu.VMEM((1, SIDE * SIDE), I32), pltpu.VMEM((HD, SEQ), BF16),
                        pltpu.VMEM((ROWS + 1, SIDE, 128), F32), pltpu.VMEM((ROWS + 1, SIDE, 128), F32),
                        pltpu.SemaphoreType.DMA((D // X_STEP,)), pltpu.SemaphoreType.DMA((3,)),
                        pltpu.SemaphoreType.DMA((4,)),
                        pltpu.SemaphoreType.DMA((2, ZS + 1))],
        compiler_params=pltpu.CompilerParams(vmem_limit_bytes=58 * 1024 * 1024),
        name="grads",
    )(layer_input[0], w_query.T, w_key.T, w_value.T, rel_bias, context_grad[0].T,
      sign_bits.transpose(1, 0, 2), dither)
    other = lax.ppermute(send, "shard", [(i, i ^ 1) for i in range(2 * ZS)])
    peaks = jnp.max(lax.all_to_all(peaks, "shard", 0, 0), axis=0)
    peaks = lax.all_to_all(jnp.broadcast_to(peaks, (GRP, 1, 128)), "grp", 0, 0)
    codes = pl.pallas_call(
        codes_kernel,
        out_shape=shaped(GRP, ROWS, 4, 128),
        in_specs=vmem(3),
        out_specs=vmem(1)[0],
        compiler_params=PARAMS,
        name="codes",
    )(mine, other, peaks)
    part = jnp.sum(lax.all_to_all(codes, "grp", 0, 0), axis=0).reshape(ZS, 3, 4, 128)
    same_core = [list(range(c, 2 * ZS, 2)) for c in (0, 1)]
    part = jnp.sum(lax.all_to_all(part, "shard", 0, 0, axis_index_groups=same_core), axis=0)
    totals = lax.all_to_all(jnp.broadcast_to(part, (GRP, 3, 4, 128)), "grp", 0, 0)
    out = pl.pallas_call(
        decode_kernel,
        out_shape=shaped(3, 2, SIDE * SIDE),
        in_specs=vmem(3),
        out_specs=vmem(1)[0],
        scratch_shapes=[pltpu.VMEM((128, 128), F32)],
        compiler_params=PARAMS,
        name="decode",
    )(totals, peaks, words)
    return out.transpose(1, 0, 2)


def solution(mesh):
    batch = P(("grp", "shard"), None, None)
    placed = (batch, P(), P(), P(), P(), batch, P(), P(("grp", "shard"), None))
    return jax.shard_map(
        per_device, mesh=mesh, in_specs=placed, out_specs=P("shard", None, None), check_vma=False
    )
```

```python
import jax
import jax.numpy as jnp
from jax import lax
from jax.experimental import pallas as pl
from jax.experimental.pallas import tpu as pltpu
from jax.sharding import PartitionSpec as P

LEVELS = 64
EPS = 1e-06
THRESHOLDS = (12, 16, 23, 32, 46, 64, 91)
SEQ, D, HD = 128, 4096, 64
SIDE = 64
GRP, ZS = 16, 16
BATCH = 512
ROWS = 3 * ZS
X_STEP = 1024
F32, BF16, I32 = jnp.float32, jnp.bfloat16, jnp.int32
NT = (((1,), (1,)), ((), ()))


def iota(shape, dim):
    return lax.broadcasted_iota(I32, shape, dim)


def parity(v):
    v = v ^ (v >> 4)
    v = v ^ (v >> 2)
    v = v ^ (v >> 1)
    return v & 1


def hadamard(size, swap=0):
    row, col = iota((size, size), 0), iota((size, size), 1)
    value = (1 - 2 * parity(row & col & (SIDE - 1))).astype(F32) * 0.125
    same = (row >> 6) == ((col >> 6) ^ (swap * 2))
    return jnp.where(same, value, 0.0).astype(BF16)


def mm(a, b):
    return jnp.dot(a, b, preferred_element_type=F32)


def terms(v, count):
    out = []
    for _ in range(count):
        part = v.astype(BF16)
        out.append(part)
        v = v - part.astype(F32)
    return out


def rotate(grid, left, right, count):
    mixed = sum(mm(t, right) for t in terms(grid, count))
    return sum(mm(left, t) for t in terms(mixed, count))


def side(group, core):
    return (group >> (2 * core)) & 1


def grads_kernel(x_ref, wq_ref, wk_ref, wv_ref, bias_in, ctx_in, bits_in, dither_in,
                 keep_ref, core_ref, near_ref, cross_ref, peaks_ref, words_ref, word_scr, peak_scr, bits_scr,
                 dither_scr, grid_scr, x_scr, w_scr, bits_ref, bias_ref, dither_ref, ctx_ref,
                 x_sem, w_sem, in_sem):
    shard = lax.axis_index("shard")
    core = shard & 1
    depth = shard >> 1
    group = lax.axis_index("grp")
    own_side, other_side = side(group, core), side(group, 1 - core)
    w_copies = [pltpu.make_async_copy(r, w_scr.at[pl.ds(HD * n, HD)], w_sem.at[n])
                for n, r in enumerate((wq_ref, wk_ref, wv_ref))]
    x_copies = [pltpu.make_async_copy(x_ref.at[:, pl.ds(n * X_STEP, X_STEP)],
                                      x_scr.at[:, pl.ds(n * X_STEP, X_STEP)], x_sem.at[n])
                for n in range(D // X_STEP)]
    small = [pltpu.make_async_copy(src, dst, in_sem.at[n]) for n, (src, dst) in enumerate(
        ((bits_in, bits_ref), (bias_in, bias_ref), (dither_in, dither_ref), (ctx_in, ctx_ref)))]
    for copy in small + w_copies + x_copies:
        copy.start()
    small[0].wait()

    for p in range(3):
        for part in (0, 1):
            bits_scr[2 * p + part] = bits_ref[p, :, part * 128:part * 128 + 128]
    rows = []
    for half in (0, 1):
        for p in range(3):
            rows.append(jnp.concatenate(
                [bits_scr[2 * p + part, pl.ds(2 * half + b, ZS, stride=4), :]
                 for b in (0, 1) for part in (0, 1)], axis=1))
    words = jnp.concatenate(rows, axis=0)
    both = jnp.concatenate([words & 255, words >> 8], axis=0).astype(F32).astype(BF16)
    row, col = iota((512, 512), 0), iota((512, 512), 1)
    source = ((col >> 6) & 1) * 256 + (col & 63) * 4 + (col >> 7)
    select = jnp.where(row == source, 1.0, 0.0).astype(BF16)
    moved = mm(both, select)
    moved = (moved[:96] + 256.0 * moved[96:]).astype(I32)
    for half in (0, 1):
        for j in range(4):
            word_scr[:, j * 256 + half * 128:j * 256 + half * 128 + 128] = (
                moved[half * 48:half * 48 + 48, j * 128:j * 128 + 128])
    for p in range(3):
        for j in range(4):
            own = word_scr[pl.ds(p * ZS + depth, 1), j * 256:j * 256 + 256]
            words_ref[p, j:j + 1, :] = jnp.where(core == 0, own[:, :128], own[:, 128:])

    for half in (0, 1):
        flipped = -jnp.where(core == half, own_side, other_side)
        for j in (2, 3):
            lanes = slice(j * 256 + half * 128, j * 256 + half * 128 + 128)
            word_scr[:, lanes] = word_scr[:, lanes] ^ flipped
    for copy in small[1:]:
        copy.wait()
    for r in range(32):
        dither_scr[r:r + 1, :] = dither_ref[:, 128 * r:128 * r + 128]
    even = dither_scr[...]
    grid_scr[pl.ds(0, 32, stride=2), :] = even
    grid_scr[pl.ds(1, 32, stride=2), :] = pltpu.roll(even, SIDE, 1)
    shift = ((grid_scr[...].astype(F32) + 0.5) * (1.0 / 65536.0)).T[:SIDE, :]
    shift = jnp.concatenate([shift, shift], axis=1)
    for chosen, refs in ((own_side, (keep_ref, near_ref)), (other_side, (core_ref, cross_ref))):
        refs[0][ROWS] = jnp.where(chosen == 0, shift[:32], shift[32:])
        refs[1][ROWS] = jnp.where(chosen == 0, shift[32:], shift[:32])

    acc = jnp.zeros((3 * HD, SEQ), F32)
    for copy in w_copies:
        copy.wait()
    for n, copy in enumerate(x_copies):
        copy.wait()
        for k in range(n * X_STEP, n * X_STEP + X_STEP, 512):
            acc = acc + lax.dot_general(w_scr[:, k:k + 512], x_scr[:, k:k + 512], NT,
                                        preferred_element_type=F32)
    queries_t, keys_t, values_t = (acc[HD * n:HD * n + HD, :].astype(BF16) for n in range(3))
    queries = acc[:HD, :].T.astype(BF16)
    upstream_t = ctx_ref[...]
    upstream = upstream_t.astype(F32).T.astype(BF16)
    offset = iota((SEQ, SEQ), 1) - iota((SEQ, SEQ), 0)
    distance = jnp.abs(offset)
    bucket = jnp.minimum(distance, 8)
    for limit in THRESHOLDS:
        bucket = bucket + (distance >= limit).astype(I32)
    bucket = bucket + jnp.where(offset > 0, 16, 0)
    bias = jnp.zeros((SEQ, SEQ), F32)
    for b in range(32):
        bias = jnp.where(bucket == b, bias_ref[b], bias)
    scores = mm(queries, keys_t) + bias
    weights = jnp.exp(scores - jnp.max(scores, axis=1, keepdims=True))
    probs = weights / jnp.sum(weights, axis=1, keepdims=True)
    prob_grad = mm(upstream, values_t)
    score_grad = (probs * (prob_grad - jnp.sum(probs * prob_grad, axis=1, keepdims=True))).astype(BF16)
    query_grad = lax.dot_general(keys_t, score_grad, NT, preferred_element_type=F32)
    key_grad = mm(queries_t, score_grad)
    value_grad = mm(upstream_t, probs.astype(BF16))
    stacked = jnp.concatenate([query_grad, key_grad, value_grad], axis=0).astype(BF16)

    left = hadamard(192)
    right = hadamard(256, core)
    bit = 31 - iota((16, 256), 0)
    for z in range(ZS):
        grid = mm(stacked, x_scr[:, 256 * z:256 * z + 256])
        signed = []
        for p in range(3):
            for j in range(4):
                line = word_scr[p * ZS + z:p * ZS + z + 1, j * 256:j * 256 + 256]
                flip = jnp.broadcast_to(line, (16, 256)) << bit
                part = grid[p * 64 + j * 16:p * 64 + j * 16 + 16, :]
                signed.append(jnp.where(flip < 0, -part, part))
        turned = rotate(jnp.concatenate(signed, axis=0), left, right, 2)
        for p in range(3):
            block = turned[p * 64:p * 64 + 64, :]
            keep_ref[3 * z + p] = block[:32, :128]
            near_ref[3 * z + p] = block[32:, :128]
            core_ref[3 * z + p] = block[:32, 128:]
            cross_ref[3 * z + p] = block[32:, 128:]
            peak_scr[3 * z + p:3 * z + p + 1, :] = jnp.max(jnp.abs(block), axis=0, keepdims=True)
    lane, line = iota((ROWS, 128), 1), iota((ROWS, 128), 0)
    for half in (0, 1):
        peaks = peak_scr[:, half * 128:half * 128 + 128]
        low = jnp.max(jnp.where(lane < 64, peaks, 0.0), axis=1, keepdims=True)
        high = jnp.max(jnp.where(lane >= 64, peaks, 0.0), axis=1, keepdims=True)
        spread = jnp.where(lane == line, low, 0.0) + jnp.where(lane - 64 == line, high, 0.0)
        packed = jnp.max(spread, axis=0, keepdims=True)
        for z in range(ZS):
            peaks_ref[2 * z + (core ^ half)] = packed


def codes_kernel(keep_ref, core_ref, near_ref, cross_ref, peaks_ref, out_ref):
    factor = LEVELS / (jnp.max(peaks_ref[...], axis=0) + EPS)
    lane, line = iota((ROWS, 128), 1), iota((ROWS, 128), 0)
    low = jnp.sum(jnp.where(lane == line, factor, 0.0), axis=1, keepdims=True)
    high = jnp.sum(jnp.where(lane - 64 == line, factor, 0.0), axis=1, keepdims=True)
    factor = jnp.where(lane < 64, low, high)
    for t in range(ROWS):
        f = factor[t:t + 1, :]
        codes = sum(jnp.floor(ref[t] * f + ref[ROWS])
                    for ref in (keep_ref, core_ref, near_ref, cross_ref))
        for q in range(8):
            out_ref[q, 4 * t:4 * t + 4, :] = codes[4 * q:4 * q + 4, :]


def sum_kernel(parts_ref, out_ref):
    total = jnp.sum(parts_ref[...], axis=0)
    for t in range(ROWS):
        out_ref[t // 3, t % 3] = total[4 * t:4 * t + 4, :]


def member(core, parity, k):
    if core == 0:
        return 4 * (k >> 1) + 2 * (k & 1) + parity
    return 4 * (2 * (k >> 2) + parity) + (k & 3)


def decode_kernel(totals_ref, peaks_ref, words_ref, out_ref, scr):
    shard = lax.axis_index("shard")
    depth, core = shard >> 1, shard & 1
    step = (jnp.max(peaks_ref[...], axis=0) + EPS) / LEVELS
    lane = iota((1, 128), 1)
    grids, signs = [], []
    bit = iota((16, 128), 0)
    for p in range(3):
        low = jnp.sum(jnp.where(lane == 3 * depth + p, step, 0.0), axis=1, keepdims=True)
        high = jnp.sum(jnp.where(lane - 64 == 3 * depth + p, step, 0.0), axis=1, keepdims=True)
        total = jnp.concatenate([totals_ref[jnp.where(core == 0, member(0, k >> 3, k & 7),
                                                      member(1, k >> 3, k & 7)), p]
                                 for k in range(GRP)], axis=0)
        grids.append(total * jnp.where(lane < 64, low, high) / BATCH)
        for j in range(4):
            word = jnp.broadcast_to(words_ref[p, j:j + 1, :], (16, 128))
            signs.append((word >> bit) & 1)
    mixed = rotate(jnp.concatenate(grids, axis=0), hadamard(192), hadamard(128), 3)
    mixed = jnp.where(jnp.concatenate(signs, axis=0) == 1, -mixed, mixed)
    for p in range(3):
        turned = mixed[64 * p:64 * p + 64, :].T
        scr[...] = jnp.concatenate([turned, turned], axis=1)
        for b in (0, 1):
            pair = [scr[pl.ds(64 * b + odd, 32, stride=2), :][:, :SIDE] for odd in (0, 1)]
            lines = jnp.concatenate(pair, axis=1)
            for r in range(32):
                out_ref[p, b:b + 1, 128 * r:128 * r + 128] = lines[r:r + 1, :]


def vmem(count):
    return [pl.BlockSpec(memory_space=pltpu.VMEM)] * count


def shaped(*shape, dtype=F32):
    return jax.ShapeDtypeStruct(shape, dtype)


PARAMS = pltpu.CompilerParams(vmem_limit_bytes=16 * 1024 * 1024)


def per_device(layer_input, w_query, w_key, w_value, rel_bias, context_grad, sign_bits, dither):
    def hbm(v):
        return pltpu.with_memory_space_constraint(v, pltpu.HBM)

    keep, to_core, to_near, to_cross, peaks, words = pl.pallas_call(
        grads_kernel,
        out_shape=[*[shaped(ROWS + 1, 32, 128)] * 4,
                   shaped(2 * ZS, 1, 128), shaped(3, 4, 128, dtype=I32)],
        in_specs=[pl.BlockSpec(memory_space=pltpu.HBM)] * 8,
        out_specs=vmem(6),
        scratch_shapes=[pltpu.VMEM((ROWS, 1024), I32), pltpu.VMEM((ROWS, 256), F32),
                        pltpu.VMEM((6, SIDE, 128), I32),
                        pltpu.VMEM((32, 128), I32), pltpu.VMEM((SIDE, 128), I32),
                        pltpu.VMEM((SEQ, D), BF16), pltpu.VMEM((3 * HD, D), BF16),
                        pltpu.VMEM((3, SIDE, 256), I32), pltpu.SMEM((32,), F32),
                        pltpu.VMEM((1, SIDE * SIDE), I32), pltpu.VMEM((HD, SEQ), BF16),
                        pltpu.SemaphoreType.DMA((D // X_STEP,)), pltpu.SemaphoreType.DMA((3,)),
                        pltpu.SemaphoreType.DMA((4,))],
        compiler_params=PARAMS,
        name="grads",
    )(*(hbm(v) for v in (layer_input[0], w_query.T, w_key.T, w_value.T, rel_bias,
                         context_grad[0].T, sign_bits.transpose(1, 0, 2), dither)))
    devices = [(g, m) for g in range(GRP) for m in range(2 * ZS)]
    everyone = ("grp", "shard")

    def swap(values, target):
        pairs = [(32 * g + m, 32 * t + u) for g, m in devices for t, u in (target(g, m),)]
        return lax.ppermute(values, everyone, pairs)

    near = swap(to_near, lambda g, m: (g ^ (1 << 2 * (m & 1)), m))
    cross = swap(to_cross, lambda g, m: (g ^ (4 >> 2 * (m & 1)), m ^ 1))
    sibling = swap(to_core, lambda g, m: (g, m ^ 1))
    peaks = jnp.max(lax.all_to_all(peaks, "shard", 0, 0), axis=0)
    peaks = lax.all_to_all(jnp.broadcast_to(peaks, (GRP, 1, 128)), "grp", 0, 0)
    codes = pl.pallas_call(
        codes_kernel,
        out_shape=shaped(8, ROWS * 4, 128),
        in_specs=vmem(5),
        out_specs=vmem(1)[0],
        compiler_params=PARAMS,
        name="codes",
    )(keep, sibling, near, cross, peaks)
    coders = [[32 * member(m & 1, parity, k) + m for k in range(8)]
              for parity in (0, 1) for m in range(2 * ZS)]
    part = pl.pallas_call(
        sum_kernel,
        out_shape=shaped(ZS, 3, 4, 128),
        in_specs=vmem(1),
        out_specs=vmem(1)[0],
        compiler_params=PARAMS,
        name="sum",
    )(lax.all_to_all(codes, everyone, 0, 0, axis_index_groups=coders))
    same_core = [list(range(c, 2 * ZS, 2)) for c in (0, 1)]
    part = jnp.sum(lax.all_to_all(part, "shard", 0, 0, axis_index_groups=same_core), axis=0)
    totals = lax.all_to_all(jnp.broadcast_to(part, (GRP, 3, 4, 128)), "grp", 0, 0)
    out = pl.pallas_call(
        decode_kernel,
        out_shape=shaped(3, 2, SIDE * SIDE),
        in_specs=vmem(3),
        out_specs=vmem(1)[0],
        scratch_shapes=[pltpu.VMEM((128, 128), F32)],
        compiler_params=PARAMS,
        name="decode",
    )(totals, peaks, words)
    return out.transpose(1, 0, 2)


def solution(mesh):
    batch = P(("grp", "shard"), None, None)
    placed = (batch, P(), P(), P(), P(), batch, P(), P(("grp", "shard"), None))
    return jax.shard_map(
        per_device, mesh=mesh, in_specs=placed, out_specs=P("shard", None, None), check_vma=False
    )
```

```python
import jax
import jax.numpy as jnp
from jax import lax
from jax.experimental import pallas as pl
from jax.experimental.pallas import tpu as pltpu
from jax.sharding import PartitionSpec as P

LEVELS = 64
EPS = 1e-06
THRESHOLDS = (12, 16, 23, 32, 46, 64, 91)
SEQ, D, HD = 128, 4096, 64
SIDE = 64
GRP, ZS = 16, 16
BATCH = 512
ROWS = 3 * ZS
X_STEP = 1024
SHIP = (5, 10, 13, 15)
F32, BF16, I32 = jnp.float32, jnp.bfloat16, jnp.int32
NT = (((1,), (1,)), ((), ()))


def iota(shape, dim):
    return lax.broadcasted_iota(I32, shape, dim)


def parity(v):
    v = v ^ (v >> 4)
    v = v ^ (v >> 2)
    v = v ^ (v >> 1)
    return v & 1


def hadamard(size, swap=0):
    row, col = iota((size, size), 0), iota((size, size), 1)
    value = (1 - 2 * parity(row & col & (SIDE - 1))).astype(F32) * 0.125
    same = (row >> 6) == ((col >> 6) ^ (swap * 2))
    return jnp.where(same, value, 0.0).astype(BF16)


def mm(a, b):
    return jnp.dot(a, b, preferred_element_type=F32)


def terms(v, count):
    out = []
    for _ in range(count):
        part = v.astype(BF16)
        out.append(part)
        v = v - part.astype(F32)
    return out


def rotate(grid, left, right, count):
    mixed = sum(mm(t, right) for t in terms(grid, count))
    return sum(mm(left, t) for t in terms(mixed, count))


def side(group, core):
    return (group >> (2 * core)) & 1


def grads_kernel(x_ref, wq_ref, wk_ref, wv_ref, bias_in, ctx_in, bits_in, dither_in,
                 keep_ref, core_out, near_out, cross_out, peaks_ref, words_ref, word_scr, peak_scr, bits_scr,
                 dither_scr, grid_scr, x_scr, w_scr, bits_ref, bias_ref, dither_ref, ctx_ref,
                 core_ref, near_ref, cross_ref, x_sem, w_sem, in_sem, out_sem):
    shard = lax.axis_index("shard")
    core = shard & 1
    depth = shard >> 1
    group = lax.axis_index("grp")
    own_side, other_side = side(group, core), side(group, 1 - core)
    w_copies = [pltpu.make_async_copy(r, w_scr.at[pl.ds(HD * n, HD)], w_sem.at[n])
                for n, r in enumerate((wq_ref, wk_ref, wv_ref))]
    x_copies = [pltpu.make_async_copy(x_ref.at[:, pl.ds(n * X_STEP, X_STEP)],
                                      x_scr.at[:, pl.ds(n * X_STEP, X_STEP)], x_sem.at[n])
                for n in range(D // X_STEP)]
    small = [pltpu.make_async_copy(src, dst, in_sem.at[n]) for n, (src, dst) in enumerate(
        ((bits_in, bits_ref), (bias_in, bias_ref), (dither_in, dither_ref), (ctx_in, ctx_ref)))]
    for copy in small + w_copies + x_copies:
        copy.start()
    small[0].wait()

    for p in range(3):
        for part in (0, 1):
            bits_scr[2 * p + part] = bits_ref[p, :, part * 128:part * 128 + 128]
    rows = []
    for half in (0, 1):
        for p in range(3):
            rows.append(jnp.concatenate(
                [bits_scr[2 * p + part, pl.ds(2 * half + b, ZS, stride=4), :]
                 for b in (0, 1) for part in (0, 1)], axis=1))
    words = jnp.concatenate(rows, axis=0)
    both = jnp.concatenate([words & 255, words >> 8], axis=0).astype(F32).astype(BF16)
    row, col = iota((512, 512), 0), iota((512, 512), 1)
    source = ((col >> 6) & 1) * 256 + (col & 63) * 4 + (col >> 7)
    select = jnp.where(row == source, 1.0, 0.0).astype(BF16)
    moved = mm(both, select)
    moved = (moved[:96] + 256.0 * moved[96:]).astype(I32)
    for half in (0, 1):
        for j in range(4):
            word_scr[:, j * 256 + half * 128:j * 256 + half * 128 + 128] = (
                moved[half * 48:half * 48 + 48, j * 128:j * 128 + 128])
    for p in range(3):
        for j in range(4):
            own = word_scr[pl.ds(p * ZS + depth, 1), j * 256:j * 256 + 256]
            words_ref[p, j:j + 1, :] = jnp.where(core == 0, own[:, :128], own[:, 128:])

    for half in (0, 1):
        flipped = -jnp.where(core == half, own_side, other_side)
        for j in (2, 3):
            lanes = slice(j * 256 + half * 128, j * 256 + half * 128 + 128)
            word_scr[:, lanes] = word_scr[:, lanes] ^ flipped
    for copy in small[1:]:
        copy.wait()
    for r in range(32):
        dither_scr[r:r + 1, :] = dither_ref[:, 128 * r:128 * r + 128]
    even = dither_scr[...]
    grid_scr[pl.ds(0, 32, stride=2), :] = even
    grid_scr[pl.ds(1, 32, stride=2), :] = pltpu.roll(even, SIDE, 1)
    shift = ((grid_scr[...].astype(F32) + 0.5) * (1.0 / 65536.0)).T[:SIDE, :]
    shift = jnp.concatenate([shift, shift], axis=1)
    for chosen, refs in ((own_side, (keep_ref, near_ref)), (other_side, (core_ref, cross_ref))):
        refs[0][0] = jnp.where(chosen == 0, shift[:32], shift[32:])
        refs[1][0] = jnp.where(chosen == 0, shift[32:], shift[:32])

    acc = jnp.zeros((3 * HD, SEQ), F32)
    for copy in w_copies:
        copy.wait()
    for n, copy in enumerate(x_copies):
        copy.wait()
        for k in range(n * X_STEP, n * X_STEP + X_STEP, 512):
            acc = acc + lax.dot_general(w_scr[:, k:k + 512], x_scr[:, k:k + 512], NT,
                                        preferred_element_type=F32)
    queries_t, keys_t, values_t = (acc[HD * n:HD * n + HD, :].astype(BF16) for n in range(3))
    queries = acc[:HD, :].T.astype(BF16)
    upstream_t = ctx_ref[...]
    upstream = upstream_t.astype(F32).T.astype(BF16)
    offset = iota((SEQ, SEQ), 1) - iota((SEQ, SEQ), 0)
    distance = jnp.abs(offset)
    bucket = jnp.minimum(distance, 8)
    for limit in THRESHOLDS:
        bucket = bucket + (distance >= limit).astype(I32)
    bucket = bucket + jnp.where(offset > 0, 16, 0)
    bias = jnp.zeros((SEQ, SEQ), F32)
    for b in range(32):
        bias = jnp.where(bucket == b, bias_ref[b], bias)
    scores = mm(queries, keys_t) + bias
    weights = jnp.exp(scores - jnp.max(scores, axis=1, keepdims=True))
    probs = weights / jnp.sum(weights, axis=1, keepdims=True)
    prob_grad = mm(upstream, values_t)
    score_grad = (probs * (prob_grad - jnp.sum(probs * prob_grad, axis=1, keepdims=True))).astype(BF16)
    query_grad = lax.dot_general(keys_t, score_grad, NT, preferred_element_type=F32)
    key_grad = mm(queries_t, score_grad)
    value_grad = mm(upstream_t, probs.astype(BF16))
    stacked = jnp.concatenate([query_grad, key_grad, value_grad], axis=0).astype(BF16)

    left = hadamard(192)
    right = hadamard(256, core)
    bit = 31 - iota((16, 256), 0)
    sent, shipped = [], 0
    for z in range(ZS):
        grid = mm(stacked, x_scr[:, 256 * z:256 * z + 256])
        signed = []
        for p in range(3):
            for j in range(4):
                line = word_scr[p * ZS + z:p * ZS + z + 1, j * 256:j * 256 + 256]
                flip = jnp.broadcast_to(line, (16, 256)) << bit
                part = grid[p * 64 + j * 16:p * 64 + j * 16 + 16, :]
                signed.append(jnp.where(flip < 0, -part, part))
        turned = rotate(jnp.concatenate(signed, axis=0), left, right, 1)
        for p in range(3):
            block = turned[p * 64:p * 64 + 64, :]
            keep_ref[3 * z + p + 1] = block[:32, :128]
            near_ref[3 * z + p + 1] = block[32:, :128]
            core_ref[3 * z + p + 1] = block[:32, 128:]
            cross_ref[3 * z + p + 1] = block[32:, 128:]
            peak_scr[3 * z + p:3 * z + p + 1, :] = jnp.max(jnp.abs(block), axis=0, keepdims=True)
        if z in SHIP:
            rows = pl.ds(shipped, 3 * z + 4 - shipped)
            for n, (src, dst) in enumerate(((core_ref, core_out), (near_ref, near_out),
                                            (cross_ref, cross_out))):
                sent.append(pltpu.make_async_copy(src.at[rows], dst.at[rows],
                                                  out_sem.at[n, SHIP.index(z)]))
                sent[-1].start()
            shipped = 3 * z + 4
    lane, line = iota((ROWS, 128), 1), iota((ROWS, 128), 0)
    for half in (0, 1):
        peaks = peak_scr[:, half * 128:half * 128 + 128]
        low = jnp.max(jnp.where(lane < 64, peaks, 0.0), axis=1, keepdims=True)
        high = jnp.max(jnp.where(lane >= 64, peaks, 0.0), axis=1, keepdims=True)
        spread = jnp.where(lane == line, low, 0.0) + jnp.where(lane - 64 == line, high, 0.0)
        packed = jnp.max(spread, axis=0, keepdims=True)
        for z in range(ZS):
            peaks_ref[2 * z + (core ^ half)] = packed
    for copy in sent:
        copy.wait()


def codes_kernel(keep_ref, core_ref, near_ref, cross_ref, peaks_ref, out_ref):
    factor = LEVELS / (jnp.max(peaks_ref[...], axis=0) + EPS)
    lane, line = iota((ROWS, 128), 1), iota((ROWS, 128), 0)
    low = jnp.sum(jnp.where(lane == line, factor, 0.0), axis=1, keepdims=True)
    high = jnp.sum(jnp.where(lane - 64 == line, factor, 0.0), axis=1, keepdims=True)
    factor = jnp.where(lane < 64, low, high)
    for t in range(ROWS):
        f = factor[t:t + 1, :]
        codes = sum(jnp.floor(ref[t + 1] * f + ref[0])
                    for ref in (keep_ref, core_ref, near_ref, cross_ref))
        for q in range(8):
            out_ref[q, 4 * t:4 * t + 4, :] = codes[4 * q:4 * q + 4, :]


def sum_kernel(parts_ref, out_ref):
    total = jnp.sum(parts_ref[...], axis=0)
    for t in range(ROWS):
        out_ref[t // 3, t % 3] = total[4 * t:4 * t + 4, :]


def member(core, parity, k):
    if core == 0:
        return 4 * (k >> 1) + 2 * (k & 1) + parity
    return 4 * (2 * (k >> 2) + parity) + (k & 3)


def decode_kernel(totals_ref, peaks_ref, words_ref, out_ref, scr):
    shard = lax.axis_index("shard")
    depth, core = shard >> 1, shard & 1
    step = (jnp.max(peaks_ref[...], axis=0) + EPS) / LEVELS
    lane = iota((1, 128), 1)
    grids, signs = [], []
    bit = iota((16, 128), 0)
    for p in range(3):
        low = jnp.sum(jnp.where(lane == 3 * depth + p, step, 0.0), axis=1, keepdims=True)
        high = jnp.sum(jnp.where(lane - 64 == 3 * depth + p, step, 0.0), axis=1, keepdims=True)
        total = jnp.concatenate([totals_ref[jnp.where(core == 0, member(0, k >> 3, k & 7),
                                                      member(1, k >> 3, k & 7)), p]
                                 for k in range(GRP)], axis=0)
        grids.append(total * jnp.where(lane < 64, low, high) / BATCH)
        for j in range(4):
            word = jnp.broadcast_to(words_ref[p, j:j + 1, :], (16, 128))
            signs.append((word >> bit) & 1)
    mixed = rotate(jnp.concatenate(grids, axis=0), hadamard(192), hadamard(128), 3)
    mixed = jnp.where(jnp.concatenate(signs, axis=0) == 1, -mixed, mixed)
    for p in range(3):
        turned = mixed[64 * p:64 * p + 64, :].T
        scr[...] = jnp.concatenate([turned, turned], axis=1)
        for b in (0, 1):
            pair = [scr[pl.ds(64 * b + odd, 32, stride=2), :][:, :SIDE] for odd in (0, 1)]
            lines = jnp.concatenate(pair, axis=1)
            for r in range(32):
                out_ref[p, b:b + 1, 128 * r:128 * r + 128] = lines[r:r + 1, :]


def vmem(count):
    return [pl.BlockSpec(memory_space=pltpu.VMEM)] * count


def shaped(*shape, dtype=F32):
    return jax.ShapeDtypeStruct(shape, dtype)


PARAMS = pltpu.CompilerParams(vmem_limit_bytes=16 * 1024 * 1024)


def per_device(layer_input, w_query, w_key, w_value, rel_bias, context_grad, sign_bits, dither):
    def hbm(v):
        return pltpu.with_memory_space_constraint(v, pltpu.HBM)

    keep, to_core, to_near, to_cross, peaks, words = pl.pallas_call(
        grads_kernel,
        out_shape=[*[shaped(ROWS + 1, 32, 128)] * 4,
                   shaped(2 * ZS, 1, 128), shaped(3, 4, 128, dtype=I32)],
        in_specs=[pl.BlockSpec(memory_space=pltpu.HBM)] * 8,
        out_specs=vmem(1) + [pl.BlockSpec(memory_space=pltpu.HBM)] * 3 + vmem(2),
        scratch_shapes=[pltpu.VMEM((ROWS, 1024), I32), pltpu.VMEM((ROWS, 256), F32),
                        pltpu.VMEM((6, SIDE, 128), I32),
                        pltpu.VMEM((32, 128), I32), pltpu.VMEM((SIDE, 128), I32),
                        pltpu.VMEM((SEQ, D), BF16), pltpu.VMEM((3 * HD, D), BF16),
                        pltpu.VMEM((3, SIDE, 256), I32), pltpu.SMEM((32,), F32),
                        pltpu.VMEM((1, SIDE * SIDE), I32), pltpu.VMEM((HD, SEQ), BF16),
                        *[pltpu.VMEM((ROWS + 1, 32, 128), F32)] * 3,
                        pltpu.SemaphoreType.DMA((D // X_STEP,)), pltpu.SemaphoreType.DMA((3,)),
                        pltpu.SemaphoreType.DMA((4,)),
                        pltpu.SemaphoreType.DMA((3, len(SHIP)))],
        compiler_params=PARAMS,
        name="grads",
    )(*(hbm(v) for v in (layer_input[0], w_query.T, w_key.T, w_value.T, rel_bias,
                         context_grad[0].T, sign_bits.transpose(1, 0, 2), dither)))
    devices = [(g, m) for g in range(GRP) for m in range(2 * ZS)]
    everyone = ("grp", "shard")

    def swap(values, target):
        pairs = [(32 * g + m, 32 * t + u) for g, m in devices for t, u in (target(g, m),)]
        return lax.ppermute(values, everyone, pairs)

    near = swap(to_near, lambda g, m: (g ^ (1 << 2 * (m & 1)), m))
    cross = swap(to_cross, lambda g, m: (g ^ (4 >> 2 * (m & 1)), m ^ 1))
    sibling = swap(to_core, lambda g, m: (g, m ^ 1))
    peaks = jnp.max(lax.all_to_all(peaks, "shard", 0, 0), axis=0)
    peaks = lax.all_to_all(jnp.broadcast_to(peaks, (GRP, 1, 128)), "grp", 0, 0)
    codes = pl.pallas_call(
        codes_kernel,
        out_shape=shaped(8, ROWS * 4, 128),
        in_specs=vmem(5),
        out_specs=vmem(1)[0],
        compiler_params=PARAMS,
        name="codes",
    )(keep, sibling, near, cross, peaks)
    coders = [[32 * member(m & 1, parity, k) + m for k in range(8)]
              for parity in (0, 1) for m in range(2 * ZS)]
    part = pl.pallas_call(
        sum_kernel,
        out_shape=shaped(ZS, 3, 4, 128),
        in_specs=vmem(1),
        out_specs=vmem(1)[0],
        compiler_params=PARAMS,
        name="sum",
    )(lax.all_to_all(codes, everyone, 0, 0, axis_index_groups=coders))
    same_core = [list(range(c, 2 * ZS, 2)) for c in (0, 1)]
    part = jnp.sum(lax.all_to_all(part, "shard", 0, 0, axis_index_groups=same_core), axis=0)
    totals = lax.all_to_all(jnp.broadcast_to(part, (GRP, 3, 4, 128)), "grp", 0, 0)
    out = pl.pallas_call(
        decode_kernel,
        out_shape=shaped(3, 2, SIDE * SIDE),
        in_specs=vmem(3),
        out_specs=vmem(1)[0],
        scratch_shapes=[pltpu.VMEM((128, 128), F32)],
        compiler_params=PARAMS,
        name="decode",
    )(totals, peaks, words)
    return out.transpose(1, 0, 2)


def solution(mesh):
    batch = P(("grp", "shard"), None, None)
    placed = (batch, P(), P(), P(), P(), batch, P(), P(("grp", "shard"), None))
    return jax.shard_map(
        per_device, mesh=mesh, in_specs=placed, out_specs=P("shard", None, None), check_vma=False
    )
```

```python
import jax
import jax.numpy as jnp
from jax import lax
from jax.experimental import pallas as pl
from jax.experimental.pallas import tpu as pltpu
from jax.sharding import PartitionSpec as P

LEVELS = 64
EPS = 1e-06
THRESHOLDS = (12, 16, 23, 32, 46, 64, 91)
SEQ, D, HD = 128, 4096, 64
SIDE = 64
GRP, ZS = 16, 16
BATCH = 512
ROWS = 3 * ZS
X_STEP = 1024
SHIP = (5, 10, 13, 15)
F32, BF16, I32 = jnp.float32, jnp.bfloat16, jnp.int32
NT = (((1,), (1,)), ((), ()))


def iota(shape, dim):
    return lax.broadcasted_iota(I32, shape, dim)


def parity(v):
    v = v ^ (v >> 4)
    v = v ^ (v >> 2)
    v = v ^ (v >> 1)
    return v & 1


def hadamard(size, swap=0):
    row, col = iota((size, size), 0), iota((size, size), 1)
    value = (1 - 2 * parity(row & col & (SIDE - 1))).astype(F32) * 0.125
    same = (row >> 6) == ((col >> 6) ^ (swap * 2))
    return jnp.where(same, value, 0.0).astype(BF16)


def mm(a, b):
    return jnp.dot(a, b, preferred_element_type=F32)


def terms(v, count):
    out = []
    for _ in range(count):
        part = v.astype(BF16)
        out.append(part)
        v = v - part.astype(F32)
    return out


def rotate(grid, left, right, count):
    mixed = sum(mm(t, right) for t in terms(grid, count))
    return sum(mm(left, t) for t in terms(mixed, count))


def side(group, core):
    return (group >> (2 * core)) & 1


def grads_kernel(x_ref, wq_ref, wk_ref, wv_ref, bias_in, ctx_in, bits_in, dither_in,
                 keep_ref, core_out, near_out, cross_out, peaks_ref, words_ref, word_scr, peak_scr, bits_scr,
                 dither_scr, grid_scr, x_scr, w_scr, bits_ref, bias_ref, dither_ref, ctx_ref,
                 core_ref, near_ref, cross_ref, x_sem, w_sem, in_sem, out_sem):
    shard = lax.axis_index("shard")
    core = shard & 1
    depth = shard >> 1
    group = lax.axis_index("grp")
    own_side, other_side = side(group, core), side(group, 1 - core)
    w_copies = [pltpu.make_async_copy(r, w_scr.at[pl.ds(HD * n, HD)], w_sem.at[n])
                for n, r in enumerate((wq_ref, wk_ref, wv_ref))]
    x_copies = [pltpu.make_async_copy(x_ref.at[:, pl.ds(n * X_STEP, X_STEP)],
                                      x_scr.at[:, pl.ds(n * X_STEP, X_STEP)], x_sem.at[n])
                for n in range(D // X_STEP)]
    small = [pltpu.make_async_copy(src, dst, in_sem.at[n]) for n, (src, dst) in enumerate(
        ((bits_in, bits_ref), (bias_in, bias_ref), (dither_in, dither_ref), (ctx_in, ctx_ref)))]
    for copy in small + w_copies + x_copies:
        copy.start()
    small[0].wait()

    for p in range(3):
        for part in (0, 1):
            bits_scr[2 * p + part] = bits_ref[p, :, part * 128:part * 128 + 128]
    rows = []
    for half in (0, 1):
        for p in range(3):
            rows.append(jnp.concatenate(
                [bits_scr[2 * p + part, pl.ds(2 * half + b, ZS, stride=4), :]
                 for b in (0, 1) for part in (0, 1)], axis=1))
    words = jnp.concatenate(rows, axis=0)
    both = jnp.concatenate([words & 255, words >> 8], axis=0).astype(F32).astype(BF16)
    row, col = iota((512, 512), 0), iota((512, 512), 1)
    source = ((col >> 6) & 1) * 256 + (col & 63) * 4 + (col >> 7)
    select = jnp.where(row == source, 1.0, 0.0).astype(BF16)
    moved = mm(both, select)
    moved = (moved[:96] + 256.0 * moved[96:]).astype(I32)
    for half in (0, 1):
        for j in range(4):
            word_scr[:, j * 256 + half * 128:j * 256 + half * 128 + 128] = (
                moved[half * 48:half * 48 + 48, j * 128:j * 128 + 128])
    for p in range(3):
        for j in range(4):
            own = word_scr[pl.ds(p * ZS + depth, 1), j * 256:j * 256 + 256]
            words_ref[p, j:j + 1, :] = jnp.where(core == 0, own[:, :128], own[:, 128:])

    for half in (0, 1):
        flipped = -jnp.where(core == half, own_side, other_side)
        for j in (2, 3):
            lanes = slice(j * 256 + half * 128, j * 256 + half * 128 + 128)
            word_scr[:, lanes] = word_scr[:, lanes] ^ flipped
    for copy in small[1:]:
        copy.wait()
    for r in range(32):
        dither_scr[r:r + 1, :] = dither_ref[:, 128 * r:128 * r + 128]
    even = dither_scr[...]
    grid_scr[pl.ds(0, 32, stride=2), :] = even
    grid_scr[pl.ds(1, 32, stride=2), :] = pltpu.roll(even, SIDE, 1)
    shift = ((grid_scr[...].astype(F32) + 0.5) * (1.0 / 65536.0)).T[:SIDE, :]
    shift = jnp.concatenate([shift, shift], axis=1)
    for chosen, refs in ((own_side, (keep_ref, near_ref)), (other_side, (core_ref, cross_ref))):
        refs[0][0] = jnp.where(chosen == 0, shift[:32], shift[32:])
        refs[1][0] = jnp.where(chosen == 0, shift[32:], shift[:32])

    acc = jnp.zeros((3 * HD, SEQ), F32)
    for copy in w_copies:
        copy.wait()
    for n, copy in enumerate(x_copies):
        copy.wait()
        for k in range(n * X_STEP, n * X_STEP + X_STEP, 512):
            acc = acc + lax.dot_general(w_scr[:, k:k + 512], x_scr[:, k:k + 512], NT,
                                        preferred_element_type=F32)
    queries_t, keys_t, values_t = (acc[HD * n:HD * n + HD, :].astype(BF16) for n in range(3))
    queries = acc[:HD, :].T.astype(BF16)
    upstream_t = ctx_ref[...]
    upstream = upstream_t.astype(F32).T.astype(BF16)
    offset = iota((SEQ, SEQ), 1) - iota((SEQ, SEQ), 0)
    distance = jnp.abs(offset)
    bucket = jnp.minimum(distance, 8)
    for limit in THRESHOLDS:
        bucket = bucket + (distance >= limit).astype(I32)
    bucket = bucket + jnp.where(offset > 0, 16, 0)
    bias = jnp.zeros((SEQ, SEQ), F32)
    for b in range(32):
        bias = jnp.where(bucket == b, bias_ref[b], bias)
    scores = mm(queries, keys_t) + bias
    weights = jnp.exp(scores - jnp.max(scores, axis=1, keepdims=True))
    probs = weights / jnp.sum(weights, axis=1, keepdims=True)
    prob_grad = mm(upstream, values_t)
    score_grad = (probs * (prob_grad - jnp.sum(probs * prob_grad, axis=1, keepdims=True))).astype(BF16)
    query_grad = lax.dot_general(keys_t, score_grad, NT, preferred_element_type=F32)
    key_grad = mm(queries_t, score_grad)
    value_grad = mm(upstream_t, probs.astype(BF16))
    stacked = jnp.concatenate([query_grad, key_grad, value_grad], axis=0).astype(BF16)

    left = hadamard(192)
    right = hadamard(256, core)
    bit = 31 - iota((16, 256), 0)
    sent, shipped = [], 0
    for first in range(0, ZS, 8):
        group = range(first, first + 8)
        grids = []
        for z in group:
            grid = mm(stacked, x_scr[:, 256 * z:256 * z + 256])
            for p in range(3):
                for j in range(4):
                    line = word_scr[p * ZS + z:p * ZS + z + 1, j * 256:j * 256 + 256]
                    flip = jnp.broadcast_to(line, (16, 256)) << bit
                    part = grid[p * 64 + j * 16:p * 64 + j * 16 + 16, :]
                    grids.append(jnp.where(flip < 0, -part, part))
        mixed = sum(mm(t, right) for t in terms(jnp.concatenate(grids, axis=0), 1))
        mixed = terms(mixed, 1)
        for n, z in enumerate(group):
            turned = sum(mm(left, t[192 * n:192 * n + 192]) for t in mixed)
            for p in range(3):
                block = turned[p * 64:p * 64 + 64, :]
                keep_ref[3 * z + p + 1] = block[:32, :128]
                near_ref[3 * z + p + 1] = block[32:, :128]
                core_ref[3 * z + p + 1] = block[:32, 128:]
                cross_ref[3 * z + p + 1] = block[32:, 128:]
                peak_scr[3 * z + p:3 * z + p + 1, :] = jnp.max(jnp.abs(block), axis=0, keepdims=True)
            if z in SHIP:
                rows = pl.ds(shipped, 3 * z + 4 - shipped)
                for n, (src, dst) in enumerate(((core_ref, core_out), (near_ref, near_out),
                                                (cross_ref, cross_out))):
                    sent.append(pltpu.make_async_copy(src.at[rows], dst.at[rows],
                                                      out_sem.at[n, SHIP.index(z)]))
                    sent[-1].start()
                shipped = 3 * z + 4
    lane, line = iota((ROWS, 128), 1), iota((ROWS, 128), 0)
    for half in (0, 1):
        peaks = peak_scr[:, half * 128:half * 128 + 128]
        low = jnp.max(jnp.where(lane < 64, peaks, 0.0), axis=1, keepdims=True)
        high = jnp.max(jnp.where(lane >= 64, peaks, 0.0), axis=1, keepdims=True)
        spread = jnp.where(lane == line, low, 0.0) + jnp.where(lane - 64 == line, high, 0.0)
        packed = jnp.max(spread, axis=0, keepdims=True)
        for z in range(ZS):
            peaks_ref[2 * z + (core ^ half)] = packed
    for copy in sent:
        copy.wait()


def codes_kernel(keep_ref, core_ref, near_ref, cross_ref, peaks_ref, out_ref):
    factor = LEVELS / (jnp.max(peaks_ref[...], axis=0) + EPS)
    lane, line = iota((ROWS, 128), 1), iota((ROWS, 128), 0)
    low = jnp.sum(jnp.where(lane == line, factor, 0.0), axis=1, keepdims=True)
    high = jnp.sum(jnp.where(lane - 64 == line, factor, 0.0), axis=1, keepdims=True)
    factor = jnp.where(lane < 64, low, high)
    for t in range(ROWS):
        f = factor[t:t + 1, :]
        codes = sum(jnp.floor(ref[t + 1] * f + ref[0])
                    for ref in (keep_ref, core_ref, near_ref, cross_ref))
        for q in range(8):
            out_ref[q, 4 * t:4 * t + 4, :] = codes[4 * q:4 * q + 4, :]


def sum_kernel(parts_ref, out_ref):
    total = jnp.sum(parts_ref[...], axis=0)
    for t in range(ROWS):
        out_ref[t // 3, t % 3] = total[4 * t:4 * t + 4, :]


def member(core, parity, k):
    if core == 0:
        return 4 * (k >> 1) + 2 * (k & 1) + parity
    return 4 * (2 * (k >> 2) + parity) + (k & 3)


def decode_kernel(totals_ref, peaks_ref, words_ref, out_ref, scr):
    shard = lax.axis_index("shard")
    depth, core = shard >> 1, shard & 1
    step = (jnp.max(peaks_ref[...], axis=0) + EPS) / LEVELS
    lane = iota((1, 128), 1)
    grids, signs = [], []
    bit = iota((16, 128), 0)
    for p in range(3):
        low = jnp.sum(jnp.where(lane == 3 * depth + p, step, 0.0), axis=1, keepdims=True)
        high = jnp.sum(jnp.where(lane - 64 == 3 * depth + p, step, 0.0), axis=1, keepdims=True)
        total = jnp.concatenate([totals_ref[jnp.where(core == 0, member(0, k >> 3, k & 7),
                                                      member(1, k >> 3, k & 7)), p]
                                 for k in range(GRP)], axis=0)
        grids.append(total * jnp.where(lane < 64, low, high) / BATCH)
        for j in range(4):
            word = jnp.broadcast_to(words_ref[p, j:j + 1, :], (16, 128))
            signs.append((word >> bit) & 1)
    mixed = rotate(jnp.concatenate(grids, axis=0), hadamard(192), hadamard(128), 3)
    mixed = jnp.where(jnp.concatenate(signs, axis=0) == 1, -mixed, mixed)
    for p in range(3):
        turned = mixed[64 * p:64 * p + 64, :].T
        scr[...] = jnp.concatenate([turned, turned], axis=1)
        for b in (0, 1):
            pair = [scr[pl.ds(64 * b + odd, 32, stride=2), :][:, :SIDE] for odd in (0, 1)]
            lines = jnp.concatenate(pair, axis=1)
            for r in range(32):
                out_ref[p, b:b + 1, 128 * r:128 * r + 128] = lines[r:r + 1, :]


def vmem(count):
    return [pl.BlockSpec(memory_space=pltpu.VMEM)] * count


def shaped(*shape, dtype=F32):
    return jax.ShapeDtypeStruct(shape, dtype)


PARAMS = pltpu.CompilerParams(vmem_limit_bytes=16 * 1024 * 1024)


def per_device(layer_input, w_query, w_key, w_value, rel_bias, context_grad, sign_bits, dither):
    def hbm(v):
        return pltpu.with_memory_space_constraint(v, pltpu.HBM)

    keep, to_core, to_near, to_cross, peaks, words = pl.pallas_call(
        grads_kernel,
        out_shape=[*[shaped(ROWS + 1, 32, 128)] * 4,
                   shaped(2 * ZS, 1, 128), shaped(3, 4, 128, dtype=I32)],
        in_specs=[pl.BlockSpec(memory_space=pltpu.HBM)] * 8,
        out_specs=vmem(1) + [pl.BlockSpec(memory_space=pltpu.HBM)] * 3 + vmem(2),
        scratch_shapes=[pltpu.VMEM((ROWS, 1024), I32), pltpu.VMEM((ROWS, 256), F32),
                        pltpu.VMEM((6, SIDE, 128), I32),
                        pltpu.VMEM((32, 128), I32), pltpu.VMEM((SIDE, 128), I32),
                        pltpu.VMEM((SEQ, D), BF16), pltpu.VMEM((3 * HD, D), BF16),
                        pltpu.VMEM((3, SIDE, 256), I32), pltpu.SMEM((32,), F32),
                        pltpu.VMEM((1, SIDE * SIDE), I32), pltpu.VMEM((HD, SEQ), BF16),
                        *[pltpu.VMEM((ROWS + 1, 32, 128), F32)] * 3,
                        pltpu.SemaphoreType.DMA((D // X_STEP,)), pltpu.SemaphoreType.DMA((3,)),
                        pltpu.SemaphoreType.DMA((4,)),
                        pltpu.SemaphoreType.DMA((3, len(SHIP)))],
        compiler_params=PARAMS,
        name="grads",
    )(*(hbm(v) for v in (layer_input[0], w_query.T, w_key.T, w_value.T, rel_bias,
                         context_grad[0].T, sign_bits.transpose(1, 0, 2), dither)))
    devices = [(g, m) for g in range(GRP) for m in range(2 * ZS)]
    everyone = ("grp", "shard")

    def swap(values, target):
        pairs = [(32 * g + m, 32 * t + u) for g, m in devices for t, u in (target(g, m),)]
        return lax.ppermute(values, everyone, pairs)

    near = swap(to_near, lambda g, m: (g ^ (1 << 2 * (m & 1)), m))
    cross = swap(to_cross, lambda g, m: (g ^ (4 >> 2 * (m & 1)), m ^ 1))
    sibling = swap(to_core, lambda g, m: (g, m ^ 1))
    peaks = jnp.max(lax.all_to_all(peaks, "shard", 0, 0), axis=0)
    peaks = lax.all_to_all(jnp.broadcast_to(peaks, (GRP, 1, 128)), "grp", 0, 0)
    codes = pl.pallas_call(
        codes_kernel,
        out_shape=shaped(8, ROWS * 4, 128),
        in_specs=vmem(5),
        out_specs=vmem(1)[0],
        compiler_params=PARAMS,
        name="codes",
    )(keep, sibling, near, cross, peaks)
    coders = [[32 * member(m & 1, parity, k) + m for k in range(8)]
              for parity in (0, 1) for m in range(2 * ZS)]
    part = pl.pallas_call(
        sum_kernel,
        out_shape=shaped(ZS, 3, 4, 128),
        in_specs=vmem(1),
        out_specs=vmem(1)[0],
        compiler_params=PARAMS,
        name="sum",
    )(lax.all_to_all(codes, everyone, 0, 0, axis_index_groups=coders))
    same_core = [list(range(c, 2 * ZS, 2)) for c in (0, 1)]
    part = jnp.sum(lax.all_to_all(part, "shard", 0, 0, axis_index_groups=same_core), axis=0)
    totals = lax.all_to_all(jnp.broadcast_to(part, (GRP, 3, 4, 128)), "grp", 0, 0)
    out = pl.pallas_call(
        decode_kernel,
        out_shape=shaped(3, 2, SIDE * SIDE),
        in_specs=vmem(3),
        out_specs=vmem(1)[0],
        scratch_shapes=[pltpu.VMEM((128, 128), F32)],
        compiler_params=PARAMS,
        name="decode",
    )(totals, peaks, words)
    return out.transpose(1, 0, 2)


def solution(mesh):
    batch = P(("grp", "shard"), None, None)
    placed = (batch, P(), P(), P(), P(), batch, P(), P(("grp", "shard"), None))
    return jax.shard_map(
        per_device, mesh=mesh, in_specs=placed, out_specs=P("shard", None, None), check_vma=False
    )
```

```python
import jax
import jax.numpy as jnp
from jax import lax
from jax.experimental import pallas as pl
from jax.experimental.pallas import tpu as pltpu
from jax.sharding import PartitionSpec as P

LEVELS = 64
EPS = 1e-06
THRESHOLDS = (12, 16, 23, 32, 46, 64, 91)
SEQ, D, HD = 128, 4096, 64
SIDE = 64
GRP, ZS = 16, 16
BATCH = 512
ROWS = 3 * ZS
X_STEP = 1024
SHIP = (5, 10, 13, 15)
F32, BF16, I32 = jnp.float32, jnp.bfloat16, jnp.int32
NT = (((1,), (1,)), ((), ()))


def iota(shape, dim):
    return lax.broadcasted_iota(I32, shape, dim)


def parity(v):
    v = v ^ (v >> 4)
    v = v ^ (v >> 2)
    v = v ^ (v >> 1)
    return v & 1


def hadamard(size, swap=0):
    row, col = iota((size, size), 0), iota((size, size), 1)
    value = (1 - 2 * parity(row & col & (SIDE - 1))).astype(F32) * 0.125
    same = (row >> 6) == ((col >> 6) ^ (swap * 2))
    return jnp.where(same, value, 0.0).astype(BF16)


def mm(a, b):
    return jnp.dot(a, b, preferred_element_type=F32)


def terms(v, count):
    out = []
    for _ in range(count):
        part = v.astype(BF16)
        out.append(part)
        v = v - part.astype(F32)
    return out


def rotate(grid, left, right, count):
    mixed = sum(mm(t, right) for t in terms(grid, count))
    return sum(mm(left, t) for t in terms(mixed, count))


def side(group, core):
    return (group >> (2 * core)) & 1


def grads_kernel(x_ref, wq_ref, wk_ref, wv_ref, bias_in, ctx_in, bits_in, dither_in,
                 keep_ref, core_out, near_out, cross_out, peaks_ref, words_ref, word_scr, peak_scr, bits_scr,
                 dither_scr, grid_scr, x_scr, w_scr, bits_ref, bias_ref, dither_ref, ctx_ref,
                 core_ref, near_ref, cross_ref, x_sem, w_sem, in_sem, out_sem):
    shard = lax.axis_index("shard")
    core = shard & 1
    depth = shard >> 1
    group = lax.axis_index("grp")
    own_side, other_side = side(group, core), side(group, 1 - core)
    w_copies = [pltpu.make_async_copy(r, w_scr.at[pl.ds(HD * n, HD)], w_sem.at[n])
                for n, r in enumerate((wq_ref, wk_ref, wv_ref))]
    x_copies = [pltpu.make_async_copy(x_ref.at[:, pl.ds(n * X_STEP, X_STEP)],
                                      x_scr.at[:, pl.ds(n * X_STEP, X_STEP)], x_sem.at[n])
                for n in range(D // X_STEP)]
    small = [pltpu.make_async_copy(src, dst, in_sem.at[n]) for n, (src, dst) in enumerate(
        ((bits_in, bits_ref), (bias_in, bias_ref), (dither_in, dither_ref), (ctx_in, ctx_ref)))]
    for copy in small + w_copies + x_copies:
        copy.start()
    small[0].wait()

    for p in range(3):
        for part in (0, 1):
            bits_scr[2 * p + part] = bits_ref[p, :, part * 128:part * 128 + 128]
    rows = []
    for half in (0, 1):
        for p in range(3):
            rows.append(jnp.concatenate(
                [bits_scr[2 * p + part, pl.ds(2 * half + b, ZS, stride=4), :]
                 for b in (0, 1) for part in (0, 1)], axis=1))
    words = jnp.concatenate(rows, axis=0)
    both = jnp.concatenate([words & 255, words >> 8], axis=0).astype(F32).astype(BF16)
    row, col = iota((512, 512), 0), iota((512, 512), 1)
    source = ((col >> 6) & 1) * 256 + (col & 63) * 4 + (col >> 7)
    select = jnp.where(row == source, 1.0, 0.0).astype(BF16)
    moved = mm(both, select)
    moved = (moved[:96] + 256.0 * moved[96:]).astype(I32)
    for half in (0, 1):
        for j in range(4):
            word_scr[:, j * 256 + half * 128:j * 256 + half * 128 + 128] = (
                moved[half * 48:half * 48 + 48, j * 128:j * 128 + 128])
    for p in range(3):
        for j in range(4):
            own = word_scr[pl.ds(p * ZS + depth, 1), j * 256:j * 256 + 256]
            words_ref[p, j:j + 1, :] = jnp.where(core == 0, own[:, :128], own[:, 128:])

    for half in (0, 1):
        flipped = -jnp.where(core == half, own_side, other_side)
        for j in (2, 3):
            lanes = slice(j * 256 + half * 128, j * 256 + half * 128 + 128)
            word_scr[:, lanes] = word_scr[:, lanes] ^ flipped
    for copy in small[1:]:
        copy.wait()
    for r in range(32):
        dither_scr[r:r + 1, :] = dither_ref[:, 128 * r:128 * r + 128]
    even = dither_scr[...]
    grid_scr[pl.ds(0, 32, stride=2), :] = even
    grid_scr[pl.ds(1, 32, stride=2), :] = pltpu.roll(even, SIDE, 1)
    shift = ((grid_scr[...].astype(F32) + 0.5) * (1.0 / 65536.0)).T[:SIDE, :]
    shift = jnp.concatenate([shift, shift], axis=1)
    for chosen, refs in ((own_side, (keep_ref, near_ref)), (other_side, (core_ref, cross_ref))):
        refs[0][0] = jnp.where(chosen == 0, shift[:32], shift[32:])
        refs[1][0] = jnp.where(chosen == 0, shift[32:], shift[:32])

    acc = jnp.zeros((3 * HD, SEQ), F32)
    for copy in w_copies:
        copy.wait()
    for n, copy in enumerate(x_copies):
        copy.wait()
        for k in range(n * X_STEP, n * X_STEP + X_STEP, 512):
            acc = acc + lax.dot_general(w_scr[:, k:k + 512], x_scr[:, k:k + 512], NT,
                                        preferred_element_type=F32)
    queries_t, keys_t, values_t = (acc[HD * n:HD * n + HD, :].astype(BF16) for n in range(3))
    queries = acc[:HD, :].T.astype(BF16)
    upstream_t = ctx_ref[...]
    upstream = upstream_t.astype(F32).T.astype(BF16)
    offset = iota((SEQ, SEQ), 1) - iota((SEQ, SEQ), 0)
    distance = jnp.abs(offset)
    bucket = jnp.minimum(distance, 8)
    for limit in THRESHOLDS:
        bucket = bucket + (distance >= limit).astype(I32)
    bucket = bucket + jnp.where(offset > 0, 16, 0)
    bias = jnp.zeros((SEQ, SEQ), F32)
    for b in range(32):
        bias = jnp.where(bucket == b, bias_ref[b], bias)
    scores = mm(queries, keys_t) + bias
    weights = jnp.exp(scores - jnp.max(scores, axis=1, keepdims=True))
    probs = weights / jnp.sum(weights, axis=1, keepdims=True)
    prob_grad = mm(upstream, values_t)
    score_grad = (probs * (prob_grad - jnp.sum(probs * prob_grad, axis=1, keepdims=True))).astype(BF16)
    query_grad = lax.dot_general(keys_t, score_grad, NT, preferred_element_type=F32)
    key_grad = mm(queries_t, score_grad)
    value_grad = mm(upstream_t, probs.astype(BF16))
    stacked = jnp.concatenate([query_grad, key_grad, value_grad], axis=0).astype(BF16)

    left = hadamard(192)
    right = hadamard(256, core)
    bit = 31 - iota((16, 256), 0)
    sent, shipped = [], 0
    for first in range(0, ZS, 16):
        group = range(first, first + 16)
        grids = []
        for z in group:
            grid = mm(stacked, x_scr[:, 256 * z:256 * z + 256])
            for p in range(3):
                for j in range(4):
                    line = word_scr[p * ZS + z:p * ZS + z + 1, j * 256:j * 256 + 256]
                    flip = jnp.broadcast_to(line, (16, 256)) << bit
                    part = grid[p * 64 + j * 16:p * 64 + j * 16 + 16, :]
                    grids.append(jnp.where(flip < 0, -part, part))
        mixed = sum(mm(t, right) for t in terms(jnp.concatenate(grids, axis=0), 1))
        mixed = terms(mixed, 1)
        for n, z in enumerate(group):
            turned = sum(mm(left, t[192 * n:192 * n + 192]) for t in mixed)
            for p in range(3):
                block = turned[p * 64:p * 64 + 64, :]
                keep_ref[3 * z + p + 1] = block[:32, :128]
                near_ref[3 * z + p + 1] = block[32:, :128]
                core_ref[3 * z + p + 1] = block[:32, 128:]
                cross_ref[3 * z + p + 1] = block[32:, 128:]
                peak_scr[3 * z + p:3 * z + p + 1, :] = jnp.max(jnp.abs(block), axis=0, keepdims=True)
            if z in SHIP:
                rows = pl.ds(shipped, 3 * z + 4 - shipped)
                for n, (src, dst) in enumerate(((core_ref, core_out), (near_ref, near_out),
                                                (cross_ref, cross_out))):
                    sent.append(pltpu.make_async_copy(src.at[rows], dst.at[rows],
                                                      out_sem.at[n, SHIP.index(z)]))
                    sent[-1].start()
                shipped = 3 * z + 4
    lane, line = iota((ROWS, 128), 1), iota((ROWS, 128), 0)
    for half in (0, 1):
        peaks = peak_scr[:, half * 128:half * 128 + 128]
        low = jnp.max(jnp.where(lane < 64, peaks, 0.0), axis=1, keepdims=True)
        high = jnp.max(jnp.where(lane >= 64, peaks, 0.0), axis=1, keepdims=True)
        spread = jnp.where(lane == line, low, 0.0) + jnp.where(lane - 64 == line, high, 0.0)
        packed = jnp.max(spread, axis=0, keepdims=True)
        for z in range(ZS):
            peaks_ref[2 * z + (core ^ half)] = packed
    for copy in sent:
        copy.wait()


def codes_kernel(keep_ref, core_ref, near_ref, cross_ref, peaks_ref, out_ref):
    factor = LEVELS / (jnp.max(peaks_ref[...], axis=0) + EPS)
    lane, line = iota((ROWS, 128), 1), iota((ROWS, 128), 0)
    low = jnp.sum(jnp.where(lane == line, factor, 0.0), axis=1, keepdims=True)
    high = jnp.sum(jnp.where(lane - 64 == line, factor, 0.0), axis=1, keepdims=True)
    factor = jnp.where(lane < 64, low, high)
    for t in range(ROWS):
        f = factor[t:t + 1, :]
        codes = sum(jnp.floor(ref[t + 1] * f + ref[0])
                    for ref in (keep_ref, core_ref, near_ref, cross_ref))
        for q in range(8):
            out_ref[q, 4 * t:4 * t + 4, :] = codes[4 * q:4 * q + 4, :]


def sum_kernel(parts_ref, out_ref):
    total = jnp.sum(parts_ref[...], axis=0)
    for t in range(ROWS):
        out_ref[t // 3, t % 3] = total[4 * t:4 * t + 4, :]


def member(core, parity, k):
    if core == 0:
        return 4 * (k >> 1) + 2 * (k & 1) + parity
    return 4 * (2 * (k >> 2) + parity) + (k & 3)


def decode_kernel(totals_ref, peaks_ref, words_ref, out_ref, scr):
    shard = lax.axis_index("shard")
    depth, core = shard >> 1, shard & 1
    step = (jnp.max(peaks_ref[...], axis=0) + EPS) / LEVELS
    lane = iota((1, 128), 1)
    grids, signs = [], []
    bit = iota((16, 128), 0)
    for p in range(3):
        low = jnp.sum(jnp.where(lane == 3 * depth + p, step, 0.0), axis=1, keepdims=True)
        high = jnp.sum(jnp.where(lane - 64 == 3 * depth + p, step, 0.0), axis=1, keepdims=True)
        total = jnp.concatenate([totals_ref[jnp.where(core == 0, member(0, k >> 3, k & 7),
                                                      member(1, k >> 3, k & 7)), p]
                                 for k in range(GRP)], axis=0)
        grids.append(total * jnp.where(lane < 64, low, high) / BATCH)
        for j in range(4):
            word = jnp.broadcast_to(words_ref[p, j:j + 1, :], (16, 128))
            signs.append((word >> bit) & 1)
    mixed = rotate(jnp.concatenate(grids, axis=0), hadamard(192), hadamard(128), 2)
    mixed = jnp.where(jnp.concatenate(signs, axis=0) == 1, -mixed, mixed)
    for p in range(3):
        turned = mixed[64 * p:64 * p + 64, :].T
        scr[...] = jnp.concatenate([turned, turned], axis=1)
        for b in (0, 1):
            pair = [scr[pl.ds(64 * b + odd, 32, stride=2), :][:, :SIDE] for odd in (0, 1)]
            lines = jnp.concatenate(pair, axis=1)
            for r in range(32):
                out_ref[p, b:b + 1, 128 * r:128 * r + 128] = lines[r:r + 1, :]


def vmem(count):
    return [pl.BlockSpec(memory_space=pltpu.VMEM)] * count


def shaped(*shape, dtype=F32):
    return jax.ShapeDtypeStruct(shape, dtype)


PARAMS = pltpu.CompilerParams(vmem_limit_bytes=16 * 1024 * 1024)


def per_device(layer_input, w_query, w_key, w_value, rel_bias, context_grad, sign_bits, dither):
    def hbm(v):
        return pltpu.with_memory_space_constraint(v, pltpu.HBM)

    keep, to_core, to_near, to_cross, peaks, words = pl.pallas_call(
        grads_kernel,
        out_shape=[*[shaped(ROWS + 1, 32, 128)] * 4,
                   shaped(2 * ZS, 1, 128), shaped(3, 4, 128, dtype=I32)],
        in_specs=[pl.BlockSpec(memory_space=pltpu.HBM)] * 8,
        out_specs=vmem(1) + [pl.BlockSpec(memory_space=pltpu.HBM)] * 3 + vmem(2),
        scratch_shapes=[pltpu.VMEM((ROWS, 1024), I32), pltpu.VMEM((ROWS, 256), F32),
                        pltpu.VMEM((6, SIDE, 128), I32),
                        pltpu.VMEM((32, 128), I32), pltpu.VMEM((SIDE, 128), I32),
                        pltpu.VMEM((SEQ, D), BF16), pltpu.VMEM((3 * HD, D), BF16),
                        pltpu.VMEM((3, SIDE, 256), I32), pltpu.SMEM((32,), F32),
                        pltpu.VMEM((1, SIDE * SIDE), I32), pltpu.VMEM((HD, SEQ), BF16),
                        *[pltpu.VMEM((ROWS + 1, 32, 128), F32)] * 3,
                        pltpu.SemaphoreType.DMA((D // X_STEP,)), pltpu.SemaphoreType.DMA((3,)),
                        pltpu.SemaphoreType.DMA((4,)),
                        pltpu.SemaphoreType.DMA((3, len(SHIP)))],
        compiler_params=PARAMS,
        name="grads",
    )(*(hbm(v) for v in (layer_input[0], w_query.T, w_key.T, w_value.T, rel_bias,
                         context_grad[0].T, sign_bits.transpose(1, 0, 2), dither)))
    devices = [(g, m) for g in range(GRP) for m in range(2 * ZS)]
    everyone = ("grp", "shard")

    def swap(values, target):
        pairs = [(32 * g + m, 32 * t + u) for g, m in devices for t, u in (target(g, m),)]
        return lax.ppermute(values, everyone, pairs)

    near = swap(to_near, lambda g, m: (g ^ (1 << 2 * (m & 1)), m))
    cross = swap(to_cross, lambda g, m: (g ^ (4 >> 2 * (m & 1)), m ^ 1))
    sibling = swap(to_core, lambda g, m: (g, m ^ 1))
    peaks = jnp.max(lax.all_to_all(peaks, "shard", 0, 0), axis=0)
    peaks = lax.all_to_all(jnp.broadcast_to(peaks, (GRP, 1, 128)), "grp", 0, 0)
    codes = pl.pallas_call(
        codes_kernel,
        out_shape=shaped(8, ROWS * 4, 128),
        in_specs=vmem(5),
        out_specs=vmem(1)[0],
        compiler_params=PARAMS,
        name="codes",
    )(keep, sibling, near, cross, peaks)
    coders = [[32 * member(m & 1, parity, k) + m for k in range(8)]
              for parity in (0, 1) for m in range(2 * ZS)]
    part = pl.pallas_call(
        sum_kernel,
        out_shape=shaped(ZS, 3, 4, 128),
        in_specs=vmem(1),
        out_specs=vmem(1)[0],
        compiler_params=PARAMS,
        name="sum",
    )(lax.all_to_all(codes, everyone, 0, 0, axis_index_groups=coders))
    same_core = [list(range(c, 2 * ZS, 2)) for c in (0, 1)]
    part = jnp.sum(lax.all_to_all(part, "shard", 0, 0, axis_index_groups=same_core), axis=0)
    totals = lax.all_to_all(jnp.broadcast_to(part, (GRP, 3, 4, 128)), "grp", 0, 0)
    out = pl.pallas_call(
        decode_kernel,
        out_shape=shaped(3, 2, SIDE * SIDE),
        in_specs=vmem(3),
        out_specs=vmem(1)[0],
        scratch_shapes=[pltpu.VMEM((128, 128), F32)],
        compiler_params=PARAMS,
        name="decode",
    )(totals, peaks, words)
    return out.transpose(1, 0, 2)


def solution(mesh):
    batch = P(("grp", "shard"), None, None)
    placed = (batch, P(), P(), P(), P(), batch, P(), P(("grp", "shard"), None))
    return jax.shard_map(
        per_device, mesh=mesh, in_specs=placed, out_specs=P("shard", None, None), check_vma=False
    )
```

```python
import jax
import jax.numpy as jnp
from jax import lax
from jax.experimental import pallas as pl
from jax.experimental.pallas import tpu as pltpu
from jax.sharding import PartitionSpec as P

LEVELS = 64
EPS = 1e-06
THRESHOLDS = (12, 16, 23, 32, 46, 64, 91)
SEQ, D, HD = 128, 4096, 64
SIDE = 64
GRP, ZS = 16, 16
BATCH = 512
ROWS = 3 * ZS
X_STEP = 1024
SHIP = (6, 11, 14, 15)
F32, BF16, I32 = jnp.float32, jnp.bfloat16, jnp.int32
NT = (((1,), (1,)), ((), ()))


def iota(shape, dim):
    return lax.broadcasted_iota(I32, shape, dim)


def parity(v):
    v = v ^ (v >> 4)
    v = v ^ (v >> 2)
    v = v ^ (v >> 1)
    return v & 1


def hadamard(size, swap=0):
    row, col = iota((size, size), 0), iota((size, size), 1)
    value = (1 - 2 * parity(row & col & (SIDE - 1))).astype(F32) * 0.125
    same = (row >> 6) == ((col >> 6) ^ (swap * 2))
    return jnp.where(same, value, 0.0).astype(BF16)


def mm(a, b):
    return jnp.dot(a, b, preferred_element_type=F32)


def terms(v, count):
    out = []
    for _ in range(count):
        part = v.astype(BF16)
        out.append(part)
        v = v - part.astype(F32)
    return out


def rotate(grid, left, right, count):
    mixed = sum(mm(t, right) for t in terms(grid, count))
    return sum(mm(left, t) for t in terms(mixed, count))


def side(group, core):
    return (group >> (2 * core)) & 1


def grads_kernel(x_ref, wq_ref, wk_ref, wv_ref, bias_in, ctx_in, bits_in, dither_in,
                 keep_ref, core_out, near_out, cross_out, peaks_ref, words_ref, word_scr, peak_scr, bits_scr,
                 dither_scr, grid_scr, x_scr, w_scr, bits_ref, bias_ref, dither_ref, ctx_ref,
                 core_ref, near_ref, cross_ref, x_sem, w_sem, in_sem, out_sem):
    shard = lax.axis_index("shard")
    core = shard & 1
    depth = shard >> 1
    group = lax.axis_index("grp")
    own_side, other_side = side(group, core), side(group, 1 - core)
    w_copies = [pltpu.make_async_copy(r, w_scr.at[pl.ds(HD * n, HD)], w_sem.at[n])
                for n, r in enumerate((wq_ref, wk_ref, wv_ref))]
    x_copies = [pltpu.make_async_copy(x_ref.at[:, pl.ds(n * X_STEP, X_STEP)],
                                      x_scr.at[:, pl.ds(n * X_STEP, X_STEP)], x_sem.at[n])
                for n in range(D // X_STEP)]
    small = [pltpu.make_async_copy(src, dst, in_sem.at[n]) for n, (src, dst) in enumerate(
        ((bits_in, bits_ref), (bias_in, bias_ref), (dither_in, dither_ref), (ctx_in, ctx_ref)))]
    for copy in small + w_copies + x_copies:
        copy.start()
    small[0].wait()

    for p in range(3):
        for part in (0, 1):
            bits_scr[2 * p + part] = bits_ref[p, :, part * 128:part * 128 + 128]
    rows = []
    for half in (0, 1):
        for p in range(3):
            rows.append(jnp.concatenate(
                [bits_scr[2 * p + part, pl.ds(2 * half + b, ZS, stride=4), :]
                 for b in (0, 1) for part in (0, 1)], axis=1))
    words = jnp.concatenate(rows, axis=0)
    both = jnp.concatenate([words & 255, words >> 8], axis=0).astype(F32).astype(BF16)
    row, col = iota((512, 512), 0), iota((512, 512), 1)
    source = ((col >> 6) & 1) * 256 + (col & 63) * 4 + (col >> 7)
    select = jnp.where(row == source, 1.0, 0.0).astype(BF16)
    moved = mm(both, select)
    moved = (moved[:96] + 256.0 * moved[96:]).astype(I32)
    for half in (0, 1):
        for j in range(4):
            word_scr[:, j * 256 + half * 128:j * 256 + half * 128 + 128] = (
                moved[half * 48:half * 48 + 48, j * 128:j * 128 + 128])
    for p in range(3):
        for j in range(4):
            own = word_scr[pl.ds(p * ZS + depth, 1), j * 256:j * 256 + 256]
            words_ref[p, j:j + 1, :] = jnp.where(core == 0, own[:, :128], own[:, 128:])

    for half in (0, 1):
        flipped = -jnp.where(core == half, own_side, other_side)
        for j in (2, 3):
            lanes = slice(j * 256 + half * 128, j * 256 + half * 128 + 128)
            word_scr[:, lanes] = word_scr[:, lanes] ^ flipped
    for copy in small[1:]:
        copy.wait()
    for r in range(32):
        dither_scr[r:r + 1, :] = dither_ref[:, 128 * r:128 * r + 128]
    even = dither_scr[...]
    grid_scr[pl.ds(0, 32, stride=2), :] = even
    grid_scr[pl.ds(1, 32, stride=2), :] = pltpu.roll(even, SIDE, 1)
    shift = ((grid_scr[...].astype(F32) + 0.5) * (1.0 / 65536.0)).T[:SIDE, :]
    shift = jnp.concatenate([shift, shift], axis=1)
    for chosen, refs in ((own_side, (keep_ref, near_ref)), (other_side, (core_ref, cross_ref))):
        refs[0][0] = jnp.where(chosen == 0, shift[:32], shift[32:])
        refs[1][0] = jnp.where(chosen == 0, shift[32:], shift[:32])

    acc = jnp.zeros((3 * HD, SEQ), F32)
    for copy in w_copies:
        copy.wait()
    for n, copy in enumerate(x_copies):
        copy.wait()
        for k in range(n * X_STEP, n * X_STEP + X_STEP, 512):
            acc = acc + lax.dot_general(w_scr[:, k:k + 512], x_scr[:, k:k + 512], NT,
                                        preferred_element_type=F32)
    queries_t, keys_t, values_t = (acc[HD * n:HD * n + HD, :].astype(BF16) for n in range(3))
    queries = acc[:HD, :].T.astype(BF16)
    upstream_t = ctx_ref[...]
    upstream = upstream_t.astype(F32).T.astype(BF16)
    offset = iota((SEQ, SEQ), 1) - iota((SEQ, SEQ), 0)
    distance = jnp.abs(offset)
    bucket = jnp.minimum(distance, 8)
    for limit in THRESHOLDS:
        bucket = bucket + (distance >= limit).astype(I32)
    bucket = bucket + jnp.where(offset > 0, 16, 0)
    bias = jnp.zeros((SEQ, SEQ), F32)
    for b in range(32):
        bias = jnp.where(bucket == b, bias_ref[b], bias)
    scores = mm(queries, keys_t) + bias
    weights = jnp.exp(scores - jnp.max(scores, axis=1, keepdims=True))
    probs = weights / jnp.sum(weights, axis=1, keepdims=True)
    prob_grad = mm(upstream, values_t)
    score_grad = (probs * (prob_grad - jnp.sum(probs * prob_grad, axis=1, keepdims=True))).astype(BF16)
    query_grad = lax.dot_general(keys_t, score_grad, NT, preferred_element_type=F32)
    key_grad = mm(queries_t, score_grad)
    value_grad = mm(upstream_t, probs.astype(BF16))
    stacked = jnp.concatenate([query_grad, key_grad, value_grad], axis=0).astype(BF16)

    left = hadamard(192)
    right = hadamard(256, core)
    bit = 31 - iota((16, 256), 0)
    sent, shipped = [], 0
    for first in range(0, ZS, 16):
        group = range(first, first + 16)
        grids = []
        for z in group:
            grid = mm(stacked, x_scr[:, 256 * z:256 * z + 256])
            for p in range(3):
                for j in range(4):
                    line = word_scr[p * ZS + z:p * ZS + z + 1, j * 256:j * 256 + 256]
                    flip = jnp.broadcast_to(line, (16, 256)) << bit
                    part = grid[p * 64 + j * 16:p * 64 + j * 16 + 16, :]
                    grids.append(jnp.where(flip < 0, -part, part))
        mixed = sum(mm(t, right) for t in terms(jnp.concatenate(grids, axis=0), 1))
        mixed = terms(mixed, 1)
        for n, z in enumerate(group):
            turned = sum(mm(left, t[192 * n:192 * n + 192]) for t in mixed)
            for p in range(3):
                block = turned[p * 64:p * 64 + 64, :]
                keep_ref[3 * z + p + 1] = block[:32, :128]
                near_ref[3 * z + p + 1] = block[32:, :128]
                core_ref[3 * z + p + 1] = block[:32, 128:]
                cross_ref[3 * z + p + 1] = block[32:, 128:]
                peak_scr[3 * z + p:3 * z + p + 1, :] = jnp.max(jnp.abs(block), axis=0, keepdims=True)
            if z in SHIP:
                rows = pl.ds(shipped, 3 * z + 4 - shipped)
                for n, (src, dst) in enumerate(((core_ref, core_out), (near_ref, near_out),
                                                (cross_ref, cross_out))):
                    sent.append(pltpu.make_async_copy(src.at[rows], dst.at[rows],
                                                      out_sem.at[n, SHIP.index(z)]))
                    sent[-1].start()
                shipped = 3 * z + 4
    lane, line = iota((ROWS, 128), 1), iota((ROWS, 128), 0)
    for half in (0, 1):
        peaks = peak_scr[:, half * 128:half * 128 + 128]
        low = jnp.max(jnp.where(lane < 64, peaks, 0.0), axis=1, keepdims=True)
        high = jnp.max(jnp.where(lane >= 64, peaks, 0.0), axis=1, keepdims=True)
        spread = jnp.where(lane == line, low, 0.0) + jnp.where(lane - 64 == line, high, 0.0)
        packed = jnp.max(spread, axis=0, keepdims=True)
        for z in range(ZS):
            peaks_ref[2 * z + (core ^ half)] = packed
    for copy in sent:
        copy.wait()


def codes_kernel(keep_ref, core_ref, near_ref, cross_ref, peaks_ref, out_ref):
    factor = LEVELS / (jnp.max(peaks_ref[...], axis=0) + EPS)
    lane, line = iota((ROWS, 128), 1), iota((ROWS, 128), 0)
    low = jnp.sum(jnp.where(lane == line, factor, 0.0), axis=1, keepdims=True)
    high = jnp.sum(jnp.where(lane - 64 == line, factor, 0.0), axis=1, keepdims=True)
    factor = jnp.where(lane < 64, low, high)
    for t in range(ROWS):
        f = factor[t:t + 1, :]
        codes = sum(jnp.floor(ref[t + 1] * f + ref[0])
                    for ref in (keep_ref, core_ref, near_ref, cross_ref))
        for q in range(8):
            out_ref[q, 4 * t:4 * t + 4, :] = codes[4 * q:4 * q + 4, :]


def sum_kernel(parts_ref, out_ref):
    total = jnp.sum(parts_ref[...], axis=0)
    for t in range(ROWS):
        out_ref[t // 3, t % 3] = total[4 * t:4 * t + 4, :]


def member(core, parity, k):
    if core == 0:
        return 4 * (k >> 1) + 2 * (k & 1) + parity
    return 4 * (2 * (k >> 2) + parity) + (k & 3)


def decode_kernel(totals_ref, peaks_ref, words_ref, out_ref, scr):
    shard = lax.axis_index("shard")
    depth, core = shard >> 1, shard & 1
    step = (jnp.max(peaks_ref[...], axis=0) + EPS) / LEVELS
    lane = iota((1, 128), 1)
    grids, signs = [], []
    bit = iota((16, 128), 0)
    for p in range(3):
        low = jnp.sum(jnp.where(lane == 3 * depth + p, step, 0.0), axis=1, keepdims=True)
        high = jnp.sum(jnp.where(lane - 64 == 3 * depth + p, step, 0.0), axis=1, keepdims=True)
        total = jnp.concatenate([totals_ref[jnp.where(core == 0, member(0, k >> 3, k & 7),
                                                      member(1, k >> 3, k & 7)), p]
                                 for k in range(GRP)], axis=0)
        grids.append(total * jnp.where(lane < 64, low, high) / BATCH)
        for j in range(4):
            word = jnp.broadcast_to(words_ref[p, j:j + 1, :], (16, 128))
            signs.append((word >> bit) & 1)
    mixed = rotate(jnp.concatenate(grids, axis=0), hadamard(192), hadamard(128), 2)
    mixed = jnp.where(jnp.concatenate(signs, axis=0) == 1, -mixed, mixed)
    for p in range(3):
        turned = mixed[64 * p:64 * p + 64, :].T
        scr[...] = jnp.concatenate([turned, turned], axis=1)
        for b in (0, 1):
            pair = [scr[pl.ds(64 * b + odd, 32, stride=2), :][:, :SIDE] for odd in (0, 1)]
            lines = jnp.concatenate(pair, axis=1)
            for r in range(32):
                out_ref[p, b:b + 1, 128 * r:128 * r + 128] = lines[r:r + 1, :]


def vmem(count):
    return [pl.BlockSpec(memory_space=pltpu.VMEM)] * count


def shaped(*shape, dtype=F32):
    return jax.ShapeDtypeStruct(shape, dtype)


PARAMS = pltpu.CompilerParams(vmem_limit_bytes=16 * 1024 * 1024)


def per_device(layer_input, w_query, w_key, w_value, rel_bias, context_grad, sign_bits, dither):
    def hbm(v):
        return pltpu.with_memory_space_constraint(v, pltpu.HBM)

    keep, to_core, to_near, to_cross, peaks, words = pl.pallas_call(
        grads_kernel,
        out_shape=[*[shaped(ROWS + 1, 32, 128)] * 4,
                   shaped(2 * ZS, 1, 128), shaped(3, 4, 128, dtype=I32)],
        in_specs=[pl.BlockSpec(memory_space=pltpu.HBM)] * 8,
        out_specs=vmem(1) + [pl.BlockSpec(memory_space=pltpu.HBM)] * 3 + vmem(2),
        scratch_shapes=[pltpu.VMEM((ROWS, 1024), I32), pltpu.VMEM((ROWS, 256), F32),
                        pltpu.VMEM((6, SIDE, 128), I32),
                        pltpu.VMEM((32, 128), I32), pltpu.VMEM((SIDE, 128), I32),
                        pltpu.VMEM((SEQ, D), BF16), pltpu.VMEM((3 * HD, D), BF16),
                        pltpu.VMEM((3, SIDE, 256), I32), pltpu.SMEM((32,), F32),
                        pltpu.VMEM((1, SIDE * SIDE), I32), pltpu.VMEM((HD, SEQ), BF16),
                        *[pltpu.VMEM((ROWS + 1, 32, 128), F32)] * 3,
                        pltpu.SemaphoreType.DMA((D // X_STEP,)), pltpu.SemaphoreType.DMA((3,)),
                        pltpu.SemaphoreType.DMA((4,)),
                        pltpu.SemaphoreType.DMA((3, len(SHIP)))],
        compiler_params=PARAMS,
        name="grads",
    )(*(hbm(v) for v in (layer_input[0], w_query.T, w_key.T, w_value.T, rel_bias,
                         context_grad[0].T, sign_bits.transpose(1, 0, 2), dither)))
    devices = [(g, m) for g in range(GRP) for m in range(2 * ZS)]
    everyone = ("grp", "shard")

    def swap(values, target):
        pairs = [(32 * g + m, 32 * t + u) for g, m in devices for t, u in (target(g, m),)]
        return lax.ppermute(values, everyone, pairs)

    near = swap(to_near, lambda g, m: (g ^ (1 << 2 * (m & 1)), m))
    cross = swap(to_cross, lambda g, m: (g ^ (4 >> 2 * (m & 1)), m ^ 1))
    sibling = swap(to_core, lambda g, m: (g, m ^ 1))
    peaks = jnp.max(lax.all_to_all(peaks, "shard", 0, 0), axis=0)
    peaks = lax.all_to_all(jnp.broadcast_to(peaks, (GRP, 1, 128)), "grp", 0, 0)
    codes = pl.pallas_call(
        codes_kernel,
        out_shape=shaped(8, ROWS * 4, 128),
        in_specs=vmem(5),
        out_specs=vmem(1)[0],
        compiler_params=PARAMS,
        name="codes",
    )(keep, sibling, near, cross, peaks)
    coders = [[32 * member(m & 1, parity, k) + m for k in range(8)]
              for parity in (0, 1) for m in range(2 * ZS)]
    part = pl.pallas_call(
        sum_kernel,
        out_shape=shaped(ZS, 3, 4, 128),
        in_specs=vmem(1),
        out_specs=vmem(1)[0],
        compiler_params=PARAMS,
        name="sum",
    )(lax.all_to_all(codes, everyone, 0, 0, axis_index_groups=coders))
    same_core = [list(range(c, 2 * ZS, 2)) for c in (0, 1)]
    part = jnp.sum(lax.all_to_all(part, "shard", 0, 0, axis_index_groups=same_core), axis=0)
    totals = lax.all_to_all(jnp.broadcast_to(part, (GRP, 3, 4, 128)), "grp", 0, 0)
    out = pl.pallas_call(
        decode_kernel,
        out_shape=shaped(3, 2, SIDE * SIDE),
        in_specs=vmem(3),
        out_specs=vmem(1)[0],
        scratch_shapes=[pltpu.VMEM((128, 128), F32)],
        compiler_params=PARAMS,
        name="decode",
    )(totals, peaks, words)
    return out.transpose(1, 0, 2)


def solution(mesh):
    batch = P(("grp", "shard"), None, None)
    placed = (batch, P(), P(), P(), P(), batch, P(), P(("grp", "shard"), None))
    return jax.shard_map(
        per_device, mesh=mesh, in_specs=placed, out_specs=P("shard", None, None), check_vma=False
    )
```
